32 devices in a mesh: groups: 2 (over x), tensor: 8 (over z, y), role: 2 (over core).
Axes of the slice: x: 2, y: 2, z: 4, core: 2. Of those that a mesh axis runs over, the one named last changes fastest.
Arguments:
- stream_in: bfloat16 [256, 8192], P(('groups', 'tensor', 'role')), parts along dimension 0, may hold values from -6 to 6
- norm_gain: bfloat16 [8192], replicated, may hold values from 0.099609375 to 1.8984375
- w_query: bfloat16 [8192, 2048], P(None, ('tensor', 'role')), may hold values from -0.0625 to 0.0625
- w_keyval: bfloat16 [8192, 512], P(None, ('tensor', 'role')), may hold values from -0.0625 to 0.0625
- w_out: bfloat16 [2048, 8192], P(('tensor', 'role')), may hold values from -0.125 to 0.125
- prefix_cache: bfloat16 [8192, 512], P(('groups', 'tensor', 'role')), parts along dimension 0, as said below
- span_lens: int32 [16], P('groups'), parts along dimension 0, may hold values from 1 to 64, 128 in all
- prefix_lens: int32 [16], P('groups'), parts along dimension 0, may hold values from 1 to 2048, 4096 in all
- owner_dev: int32 [16], P('groups'), parts along dimension 0, may hold values from 0 to 15, as said below
- offsets: int32 [16], P('groups'), parts along dimension 0, may hold values from 0 to 384
- decode_cache: bfloat16 [16384, 512], P(('groups', 'tensor', 'role')), parts along dimension 0, may hold values from -6 to 6
Outputs:
- stream_out: bfloat16 [256, 8192], P(('groups', 'tensor', 'role')), parts along dimension 0
- cache_out: bfloat16 [16384, 512], P(('groups', 'tensor', 'role')), parts along dimension 0
The draws below stay inside these ranges and needn't reach their ends.
There are 2 independent parts, one for each index of `groups`. The reference program is written for one: setup_inputs(seed, part) draws one part's arguments, and reference() takes and returns one part's arrays. A program takes and returns all parts, laid end to end along the dimension named above; an argument that names none is the same for every part. Nothing has to cross between parts.
Inputs may be any that keep to these rules, and one draw needn't show every extreme that they name: `owner_dev`: the owners are distinct device indices. `prefix_cache`: a few prefix keys may be of large magnitude.
All inputs are finite; a program needn't handle non-finite values.
Results may differ from the reference program's by a relative error of at most 0.012.
The reference program's roundings to bfloat16 on the way count: a program that leaves them out, or rounds other values in their place, can miss the bound.
Values may be sent and summed in bfloat16 or wider, within the bound.
A program may use at most 128 MiB of HBM per device.

```python
import math
import jax
import jax.numpy as jnp
import numpy as np
from jax import lax

D = 8192
HEAD = 128
GROUP = 8
CH = 128
CACHE_DEV = 512
SEQS = 8
HEADS = 16
KV_HEADS = 2
KVW = 512
PRE = 4096


def draw_prefix_cache(key, part):
    key = jax.random.fold_in(key, 5)
    row_width = KV_HEADS * 2 * HEAD
    values = jax.random.normal(key, (PRE, row_width), jnp.float32)
    values = jnp.clip(values, -6.0, 6.0)
    return values.astype(jnp.bfloat16)


def draw_owner_dev(key, part):
    key = jax.random.fold_in(key, 1)
    shuffled = jax.random.permutation(key, HEADS)
    return shuffled[:SEQS].astype(jnp.int32)


def draw_offsets(key, part):
    key = jax.random.fold_in(key, 2)
    starts = jax.random.randint(key, (SEQS,), 0, CACHE_DEV - CH + 1)
    starts = starts.at[0].set(CACHE_DEV - CH).at[1].set(0)
    return starts.astype(jnp.int32)


def block_levels(stream_key, dims, cuts, smallest, largest):
    factor_of, own = 1.0, jax.random.fold_in(stream_key, 6)
    for dim, parts in cuts:
        heights = jnp.exp(jax.random.uniform(jax.random.fold_in(own, dim), (parts,), jnp.float32, smallest / len(cuts), largest / len(cuts)))
        factor_of = factor_of * jnp.repeat(heights, dims[dim] // parts).reshape([-1 if axis == dim else 1 for axis in range(len(dims))])
    return factor_of


def length_profile(amount, total, bound, skew):
    portions = [(1 << 20) // math.isqrt(grade ** skew) + 1 for grade in range(2, amount + 1)]
    spare, holding = total - bound - (amount - 1), [1] * (amount - 1)
    while spare > 0:
        free = [i for i in range(amount - 1) if holding[i] < bound]
        mass, left = sum([portions[i] for i in free]), spare
        for i in free:
            extra = min(bound - holding[i], max(1, left * portions[i] // mass), spare)
            holding[i] = holding[i] + extra
            spare = spare - extra
    return np.array([bound] + holding)


def ragged(rng, count, total, most, lean):
    if count == 2:
        one = jax.random.randint(rng, (), max(1, total - most), min(most, total - 1) + 1)
        return jnp.stack([one, total - one])
    sizes = jnp.asarray(length_profile(count, total, most, lean), jnp.int32)
    pairs = (count - 1) // 2
    source_of, receiver = sizes[1:1 + 2 * pairs:2], sizes[2:2 + 2 * pairs:2]
    room = jnp.minimum(source_of - 1, most - receiver)
    passed = jax.random.randint(jax.random.fold_in(rng, 1), (pairs,), 0, 1 << 20) % (room + 1)
    sizes = sizes.at[1:1 + 2 * pairs:2].set(source_of - passed).at[2:2 + 2 * pairs:2].set(receiver + passed)
    return sizes[jax.random.permutation(jax.random.fold_in(rng, 2), count)]


def scatter_about(stream_key, dims, spread, limit, cuts=(), kind=jnp.bfloat16):
    entries = jax.random.normal(stream_key, dims, jnp.float32) * spread
    if len(cuts) > 0:
        entries = block_levels(stream_key, dims, cuts, -0.22, 0.18) * entries
    return jnp.clip(entries, min=-limit, max=limit).astype(kind)


def setup_inputs(seed: int = 0, part: int = 0) -> dict:
    seeds = jax.random.split(jax.random.key(seed), 12)
    own_keys = jax.random.split(jax.random.fold_in(seeds[11], part), 12)
    return {
        "stream_in": scatter_about(own_keys[0], (CH, D), 1.0, 6.0, ((0, 16),)),
        "norm_gain": jnp.clip(1.0 + 0.18 * jax.random.normal(seeds[1], (D,), jnp.float32), 0.099609375, 1.8984375).astype(jnp.bfloat16),
        "w_query": scatter_about(seeds[2], (D, HEADS * HEAD), D ** -0.5, 0.0625, ((1, 16),)),
        "w_keyval": scatter_about(seeds[3], (D, KVW), D ** -0.5, 0.0625, ((1, 16),)),
        "w_out": scatter_about(seeds[4], (HEADS * HEAD, D), (HEADS * HEAD) ** -0.5, 0.125, ((0, 16),)),
        "prefix_cache": draw_prefix_cache(jax.random.fold_in(jax.random.fold_in(seeds[11], part), 71), part),
        "span_lens": ragged(own_keys[6], SEQS, CH, CH // 2, 2).astype(jnp.int32),
        "prefix_lens": ragged(own_keys[7], SEQS, PRE, PRE // 2, 2).astype(jnp.int32),
        "owner_dev": draw_owner_dev(jax.random.fold_in(jax.random.fold_in(seeds[11], part), 71), part),
        "offsets": draw_offsets(jax.random.fold_in(jax.random.fold_in(seeds[11], part), 71), part),
        "decode_cache": scatter_about(own_keys[10], (HEADS * CACHE_DEV, KVW), 1.0, 6.0, ((0, 16),)),
    }


epsilon = 1e-05
negative = -1e+30

def segment_of(positions, lengths):
    run_ends = jnp.cumsum(lengths).astype(jnp.int32)
    return lax.optimization_barrier(jnp.sum((positions[:, None] >= run_ends[None, :]).astype(jnp.int32), axis=1))

def reference(stream_in, norm_gain, w_query, w_keyval, w_out, prefix_cache, span_lens, prefix_lens, owner_dev, offsets, decode_cache):
    floats = stream_in.astype(jnp.float32)
    normed = (floats * lax.rsqrt(lax.optimization_barrier(jnp.mean(floats * floats, axis=1, keepdims=True)) + epsilon) * norm_gain.astype(jnp.float32)).astype(jnp.bfloat16)
    queries = jnp.dot(normed, w_query, preferred_element_type=jnp.float32).astype(jnp.bfloat16)
    keyval = jnp.dot(normed, w_keyval, preferred_element_type=jnp.float32).astype(jnp.bfloat16)
    tok_seg = segment_of(jnp.arange(CH, dtype=jnp.int32), span_lens)
    pre_seg = segment_of(jnp.arange(PRE, dtype=jnp.int32), prefix_lens)
    row_index = jnp.arange(CH, dtype=jnp.int32)
    span_mask = (tok_seg[:, None] == tok_seg[None, :]) & (row_index[:, None] >= row_index[None, :])
    pre_mask = tok_seg[:, None] == pre_seg[None, :]
    visible = jnp.concatenate([pre_mask, span_mask], axis=1)
    score_scale = 1.0 / HEAD ** 0.5

    def one_head(head_index):
        column_base = head_index // GROUP * (2 * HEAD)
        query_rows = lax.dynamic_slice_in_dim(queries, head_index * HEAD, HEAD, 1)
        key_rows = jnp.concatenate([lax.dynamic_slice_in_dim(prefix_cache, column_base, HEAD, 1), lax.dynamic_slice_in_dim(keyval, column_base, HEAD, 1)], axis=0)
        value_rows = jnp.concatenate([lax.dynamic_slice_in_dim(prefix_cache, column_base + HEAD, HEAD, 1), lax.dynamic_slice_in_dim(keyval, column_base + HEAD, HEAD, 1)], axis=0)
        scores = jnp.dot(query_rows, key_rows.T, preferred_element_type=jnp.float32) * score_scale
        scores = jnp.where(visible, scores, negative)
        row_max = lax.optimization_barrier(jnp.max(scores, axis=1, keepdims=True))
        weights = jnp.where(visible, jnp.exp(scores - row_max), 0.0)
        row_total = lax.optimization_barrier(jnp.sum(weights, axis=1, keepdims=True))
        summed = jnp.dot(weights.astype(jnp.bfloat16), value_rows, preferred_element_type=jnp.float32)
        return (summed / row_total).astype(jnp.bfloat16)
    heads_out = lax.map(one_head, jnp.arange(HEADS, dtype=jnp.int32))
    attention = jnp.transpose(heads_out, (1, 0, 2)).reshape(CH, HEADS * HEAD)
    stream_out = (floats + jnp.dot(attention, w_out, preferred_element_type=jnp.float32)).astype(jnp.bfloat16)
    updated = decode_cache
    padded = jnp.concatenate([keyval, jnp.zeros((CH, KVW), jnp.bfloat16)], axis=0)
    starts = (jnp.cumsum(span_lens) - span_lens).astype(jnp.int32)
    for request in range(SEQS):
        kv_block = lax.dynamic_slice_in_dim(padded, starts[request], CH, 0)
        first_row = (owner_dev[request] * CACHE_DEV + offsets[request]).astype(jnp.int32)
        before = lax.dynamic_slice_in_dim(updated, first_row, CH, 0)
        written = jnp.where((row_index < span_lens[request])[:, None], kv_block, before)
        updated = lax.dynamic_update_slice_in_dim(updated, written, first_row, 0)
    return (stream_out, updated)
```

```python
import jax
import jax.numpy as jnp
from jax import lax
from jax.experimental import pallas as pl
from jax.experimental.pallas import tpu as pltpu
from jax.sharding import PartitionSpec as P

HEAD = 128
GROUP = 8


epsilon = 1e-05
negative = -1e30


def segment_of(positions, lengths):
    run_ends = jnp.cumsum(lengths)
    return jnp.sum((positions[:, None] >= run_ends[None, :]).astype(jnp.int32), axis=1)


def shards(
    stream_in,
    norm_gain,
    w_query,
    w_keyval,
    w_out,
    prefix_cache,
    span_lens,
    prefix_lens,
    owner_dev,
    offsets,
    decode_cache,
):
    devices = lax.axis_size(("tensor", "role"))
    myself = lax.axis_index(("tensor", "role"))
    span_rows = stream_in.shape[0] * devices
    local_pre = prefix_cache.shape[0]
    kv_heads = devices // GROUP
    score_scale = 1.0 / HEAD**0.5
    floats = stream_in.astype(jnp.float32)
    normed = (
        floats
        * lax.rsqrt(jnp.mean(floats * floats, axis=1, keepdims=True) + epsilon)
        * norm_gain.astype(jnp.float32)
    ).astype(jnp.bfloat16)
    shard_rows = lax.all_gather(normed, ("tensor", "role"), axis=0, tiled=True)
    projected = jnp.concatenate(
        [
            jnp.dot(shard_rows, w_query, preferred_element_type=jnp.float32),
            jnp.dot(shard_rows, w_keyval, preferred_element_type=jnp.float32),
        ],
        axis=1,
    )
    queries = projected[:, :HEAD].astype(jnp.bfloat16)
    kv_local = projected[:, HEAD:].astype(jnp.bfloat16)
    keyval = lax.all_gather(kv_local, ("tensor", "role"), axis=1, tiled=True)
    column_base = myself // GROUP * (2 * HEAD)
    span_keys = lax.dynamic_slice_in_dim(keyval, column_base, HEAD, 1)
    span_values = lax.dynamic_slice_in_dim(keyval, column_base + HEAD, HEAD, 1)
    row_index = jnp.arange(span_rows, dtype=jnp.int32)
    tok_seg = segment_of(row_index, span_lens)
    span_mask = (tok_seg[:, None] == tok_seg[None, :]) & (row_index[:, None] >= row_index[None, :])
    span_scores = jnp.where(
        span_mask,
        jnp.dot(queries, span_keys.T, preferred_element_type=jnp.float32) * score_scale,
        negative,
    )
    stored = jnp.transpose(prefix_cache.reshape(local_pre, kv_heads, 2 * HEAD), (1, 0, 2))
    span_max = jnp.max(span_scores, axis=1)
    span_weights = jnp.where(span_mask, jnp.exp(span_scores - span_max[:, None]), 0.0)
    start_carry = (
        span_max,
        jnp.sum(span_weights, axis=1),
        jnp.dot(span_weights.astype(jnp.bfloat16), span_values, preferred_element_type=jnp.float32),
    )
    repeated = jnp.repeat(stored, GROUP, axis=0)
    received = lax.all_to_all(repeated, ("tensor", "role"), split_axis=0, concat_axis=1, tiled=True)
    all_rows = devices * local_pre
    factor_count = 1
    while devices % (factor_count * 2) == 0 and factor_count * 2 * local_pre <= 512:
        factor_count = factor_count * 2
    block_rows = factor_count * local_pre
    blocks = received.reshape(all_rows // block_rows, block_rows, 2 * HEAD)

    def absorb(running, block_pair):
        row_max, row_total, summed = running
        block_number, shard_rows = block_pair
        row_start = block_number * block_rows
        key_seg = segment_of(row_start + jnp.arange(block_rows, dtype=jnp.int32), prefix_lens)
        visible = tok_seg[:, None] == key_seg[None, :]
        key_rows = shard_rows[:, :HEAD]
        value_rows = shard_rows[:, HEAD:]
        scores = jnp.where(
            visible,
            jnp.dot(queries, key_rows.T, preferred_element_type=jnp.float32) * score_scale,
            negative,
        )
        new_max = jnp.maximum(row_max, jnp.max(scores, axis=1))
        factor = jnp.exp(row_max - new_max)
        weights = jnp.where(visible, jnp.exp(scores - new_max[:, None]), 0.0)
        summed = summed * factor[:, None] + jnp.dot(
            weights.astype(jnp.bfloat16), value_rows, preferred_element_type=jnp.float32
        )
        return ((new_max, row_total * factor + jnp.sum(weights, axis=1), summed), None)

    numbers = jnp.arange(all_rows // block_rows, dtype=jnp.int32)
    (row_max, row_total, summed), unused = lax.scan(absorb, start_carry, (numbers, blocks))
    attention = (summed / row_total[:, None]).astype(jnp.bfloat16)
    stream_out = (
        floats
        + lax.psum_scatter(
            jnp.dot(attention, w_out, preferred_element_type=jnp.float32),
            ("tensor", "role"),
            scatter_dimension=0,
            tiled=True,
        )
    ).astype(jnp.bfloat16)
    owned = owner_dev == myself
    owned_count = jnp.sum(owned.astype(jnp.int32))
    starts = jnp.cumsum(span_lens) - span_lens
    first_row = jnp.sum(jnp.where(owned, starts, 0))
    length = jnp.sum(jnp.where(owned, span_lens, 0))
    target = jnp.sum(jnp.where(owned, offsets, 0))
    padded = jnp.concatenate(
        [keyval, jnp.zeros((span_rows, keyval.shape[1]), jnp.bfloat16)], axis=0
    )
    kv_block = lax.dynamic_slice_in_dim(padded, first_row, span_rows, 0)
    before = lax.dynamic_slice_in_dim(decode_cache, target, span_rows, 0)
    keep_new = (row_index < length) & (owned_count > 0)
    written = jnp.where(keep_new[:, None], kv_block, before)
    cache_out = lax.dynamic_update_slice_in_dim(decode_cache, written, target, 0)
    return (stream_out, cache_out)


MESH = pl.DeviceIdType.MESH
F32 = jnp.float32
BF16 = jnp.bfloat16
CW, CCW = 0, 1


def chip_at(position, chips):
    back = position // (chips // 2)
    return (1 - back) * 2 * position + back * (2 * (chips - 1 - position) + 1)


def fused(
    x_ref,
    gain_ref,
    span_ref,
    plen_ref,
    owner_ref,
    offset_ref,
    wq_hbm,
    wkv_hbm,
    wout_hbm,
    pre_hbm,
    dec_hbm,
    out_ref,
    cache_ref,
    wq,
    wkv,
    wout,
    dec,
    normed,
    xsend,
    xrecv,
    kvbuf,
    kvt,
    scores,
    part,
    peer_out,
    peer_in,
    ring_out,
    ring_in,
    lsem,
    xs,
    xr,
    ags,
    agr,
    pfs,
    pfr,
    p1s,
    p1r,
    p2s,
    p2r,
    pps,
    ppr,
    kvs,
    kvr,
    pes,
    per,
    rss,
    rsr,
):
    chips = lax.axis_size("tensor")
    devices = 2 * chips
    t = lax.axis_index("tensor")
    c = lax.axis_index("role")
    peer = 1 - c
    d = 2 * t + c
    odd = t % 2
    pos = (1 - odd) * (t // 2) + odd * (chips - 1 - t // 2)
    nxt = chip_at((pos + 1) % chips, chips)
    prv = chip_at((pos + chips - 1) % chips, chips)
    width = x_ref.shape[1]
    half = width // 2
    quarter = width // 4
    tokens = 16 * chips
    pre_rows = pre_hbm.shape[0]
    all_pre = devices * pre_rows
    g = t // 4
    u = t % 4

    def remote(src, dst, ssem, rsem, tt, cc):
        return pltpu.make_async_remote_copy(
            src_ref=src,
            dst_ref=dst,
            send_sem=ssem,
            recv_sem=rsem,
            device_id={"tensor": tt, "role": cc},
            device_id_type=MESH,
        )

    sent = []

    def send(*args):
        copy = remote(*args)
        copy.start()
        sent.append(copy)

    barrier = pltpu.get_barrier_semaphore()
    for r in range(1, devices):
        other = (d + r) % devices
        pl.semaphore_signal(
            barrier, inc=1, device_id={"tensor": other // 2, "role": other % 2}, device_id_type=MESH
        )

    def pre_slot(index):
        return kvbuf.at[pl.ds(pl.multiple_of(index * pre_rows, pre_rows), pre_rows), :]

    def head_columns(head):
        return pre_hbm.at[:, pl.ds(pl.multiple_of(head * 2 * HEAD, 2 * HEAD), 2 * HEAD)]

    loads = [
        pltpu.make_async_copy(head_columns(g), pre_slot(d), lsem.at[0]),
        pltpu.make_async_copy(wkv_hbm, wkv, lsem.at[1]),
        pltpu.make_async_copy(wq_hbm, wq, lsem.at[2]),
        pltpu.make_async_copy(wout_hbm, wout, lsem.at[3]),
        pltpu.make_async_copy(dec_hbm, dec, lsem.at[4]),
    ]
    for load in loads:
        load.start()

    floats = x_ref[...].astype(F32)
    mine = floats * lax.rsqrt(jnp.mean(floats * floats, axis=1, keepdims=True) + epsilon)
    mine = mine * gain_ref[...].astype(F32)
    is_one = (c == 1).astype(F32)
    left, right = mine[:, :half], mine[:, half:]
    xsend[...] = jnp.where(is_one > 0.5, left, right).astype(BF16)
    kept = jnp.where(is_one > 0.5, right, left).astype(BF16).astype(F32)

    pl.semaphore_wait(barrier, devices - 1)
    send(xsend, xrecv, xs, xr, t, peer)

    def block(chip, core, h=None):
        column = core * half if h is None else core * half + h * quarter
        size = half if h is None else quarter
        return (
            pl.ds(pl.multiple_of(16 * chip, 16), 16),
            pl.ds(pl.multiple_of(column, quarter), size),
        )

    remote(xsend, xrecv, xs, xr, t, peer).wait_recv()
    theirs = xrecv[...].astype(F32)
    first = jnp.where(is_one > 0.5, theirs, kept)
    second = jnp.where(is_one > 0.5, kept, theirs)
    normed[block(t, c)] = jnp.concatenate([first, second], axis=0).astype(BF16)

    def source(way, hops):
        return chip_at((pos + chips - hops) % chips if way == CW else (pos + hops) % chips, chips)

    def hop(way, s, h):
        here = normed.at[block(source(way, s), c, h)]
        send(here, here, ags.at[way, s, h], agr.at[way, s, h], (nxt, prv)[way], c)

    last = chips // 2 - 1
    own = normed.at[block(t, c)]
    messages = [(s, h, way) for s in range(last + 1) for h in range(2) for way in (CW, CCW)]
    messages = [m for m in messages if m[0] < last or m[1] == m[2]]
    for s, h, way in messages:
        if s == 0:
            hop(way, 0, h)
    send(own, own, pfs.at[0, last, 1], pfr.at[0, last, 1], t, peer)
    for s, h, way in messages:
        landed = normed.at[block(source(way, s + 1), c, h)]
        remote(landed, landed, ags.at[way, s, h], agr.at[way, s, h], nxt, c).wait_recv()
        if (s + 1, h, way) in messages:
            hop(way, s + 1, h)
        send(landed, landed, pfs.at[way, s, h], pfr.at[way, s, h], t, peer)
        if (s, h, way) == messages[1]:
            other_half = (t + 4) % chips
            send(
                head_columns(1 - g), pre_slot(d), p1s, p1r, other_half, c
            )

    loads[0].wait()
    partner = 2 * ((t + 4) % chips) + c

    def spread(index, which):
        for j in range(1, 4):
            send(pre_slot(index), pre_slot(index), p2s.at[j, which], p2r.at[j, which], 4 * g + (u + j) % 4, c)
        send(pre_slot(index), pre_slot(index), pps.at[0, which], ppr.at[0, which], t, peer)

    spread(d, 0)
    remote(pre_slot(partner), pre_slot(partner), p1s, p1r, t, peer).wait_recv()
    spread(partner, 1)

    own = normed.at[block(t, peer)]
    remote(own, own, pfs.at[0, last, 1], pfr.at[0, last, 1], t, peer).wait_recv()
    for s, h, way in messages:
        landed = normed.at[block(source(way, s + 1), peer, h)]
        remote(landed, landed, pfs.at[way, s, h], pfr.at[way, s, h], t, peer).wait_recv()
    loads[1].wait()
    kv = jnp.dot(normed[...], wkv[...], preferred_element_type=F32)
    kv_rows = wkv.shape[1]

    def kv_slot(index):
        return kvt.at[pl.ds(pl.multiple_of(index * kv_rows, kv_rows), kv_rows), :]

    kv_slot(d)[...] = jnp.transpose(kv).astype(BF16)
    for r in range(1, devices):
        other = (d + r) % devices
        send(kv_slot(d), kv_slot(d), kvs.at[r], kvr.at[r], other // 2, other % 2)
    loads[2].wait()
    queries = jnp.dot(normed[...], wq[...], preferred_element_type=F32).astype(BF16)

    def segments(positions, ref):
        end = 0
        total = jnp.zeros_like(positions)
        for r in range(ref.shape[0]):
            end = end + ref[r]
            total = total + (positions >= end).astype(jnp.int32)
        return total

    tok_col = segments(lax.broadcasted_iota(jnp.int32, (tokens, 1), 0), span_ref)
    tok_row = segments(lax.broadcasted_iota(jnp.int32, (1, tokens), 1), span_ref)

    for which in range(2):
        for j in range(1, 4):
            chip = 4 * g + (u + 4 - j) % 4
            chip = chip if which == 0 else (chip + 4) % chips
            slot = pre_slot(2 * chip + c)
            remote(slot, slot, p2s.at[j, which], p2r.at[j, which], t, peer).wait_recv()
            send(slot, slot, pps.at[j, which], ppr.at[j, which], t, peer)
    for r in range(1, devices):
        slot = kv_slot((d + devices - r) % devices)
        remote(slot, slot, kvs.at[r], kvr.at[r], t, peer).wait_recv()
    score_scale = 1.0 / HEAD**0.5
    key_base = pl.multiple_of(g * 2 * HEAD, 2 * HEAD)
    span_keys = kvt[pl.ds(key_base, HEAD), :]
    span_values = kvt[pl.ds(key_base + HEAD, HEAD), :]
    before = lax.broadcasted_iota(jnp.int32, (tokens, tokens), 0) >= lax.broadcasted_iota(
        jnp.int32, (tokens, tokens), 1
    )
    span_mask = (tok_col == tok_row) & before
    span_scores = jnp.where(
        span_mask, jnp.dot(queries, span_keys, preferred_element_type=F32) * score_scale, negative
    )
    for which in range(2):
        for j in range(4):
            chip = 4 * g + (u + 4 - j) % 4
            chip = chip if which == 0 else (chip + 4) % chips
            slot = pre_slot(2 * chip + peer)
            remote(slot, slot, pps.at[j, which], ppr.at[j, which], t, peer).wait_recv()

    tile = 512
    nt = (((1,), (1,)), ((), ()))
    seen = []
    row_max = jnp.max(span_scores, axis=1, keepdims=True)
    for i in range(all_pre // tile):
        place = lax.broadcasted_iota(jnp.int32, (1, tile), 1) + i * tile
        seg = segments(place, plen_ref)
        seen.append(seg)
        raw = lax.dot_general(
            queries, kvbuf[i * tile : (i + 1) * tile, :HEAD], nt, preferred_element_type=F32
        )
        masked = jnp.where(tok_col == seg, raw * score_scale, negative)
        scores[:, i * tile : (i + 1) * tile] = masked
        row_max = jnp.maximum(row_max, jnp.max(masked, axis=1, keepdims=True))
    weights = jnp.where(span_mask, jnp.exp(span_scores - row_max), 0.0)
    row_total = jnp.sum(weights, axis=1, keepdims=True)
    summed = lax.dot_general(weights.astype(BF16), span_values, nt, preferred_element_type=F32)
    for i in range(all_pre // tile):
        weights = jnp.exp(scores[:, i * tile : (i + 1) * tile] - row_max)
        weights = jnp.where(tok_col == seen[i], weights, 0.0)
        row_total = row_total + jnp.sum(weights, axis=1, keepdims=True)
        summed = summed + jnp.dot(
            weights.astype(BF16),
            kvbuf[i * tile : (i + 1) * tile, HEAD:],
            preferred_element_type=F32,
        )
    attention = (summed / row_total).astype(BF16)

    loads[3].wait()
    step = 1024
    for i in range(width // step):
        part[:, i * step : (i + 1) * step] = jnp.dot(
            attention, wout[:, i * step : (i + 1) * step], preferred_element_type=F32
        )

    def stacked(k, core, h):
        rows = pl.ds(pl.multiple_of(16 * chip_at((pos + k) % chips, chips) + 8 * core, 8), 8)
        top = part[rows, h * quarter : (h + 1) * quarter]
        bottom = part[rows, half + h * quarter : half + (h + 1) * quarter]
        return jnp.concatenate([top, bottom], axis=0)

    order = [4, 3, 5, 2, 6, 1, 7, 0]
    for k in order:
        for h in range(2):
            peer_out[k, :, h * quarter : (h + 1) * quarter] = stacked(k, peer, h).astype(BF16)
        send(peer_out.at[k], peer_in.at[k], pes.at[k], per.at[k], t, peer)

    def summand(k, h):
        return stacked(k, c, h) + peer_in[k, :, h * quarter : (h + 1) * quarter].astype(F32)

    def from_peer(k):
        remote(peer_out.at[k], peer_in.at[k], pes.at[k], per.at[k], t, peer).wait_recv()

    def from_ring(way, s, h):
        remote(
            ring_out.at[way, s, h], ring_in.at[way, s, h], rss.at[way, s, h], rsr.at[way, s, h], nxt, c
        ).wait_recv()
        return ring_in[way, s, h].astype(F32)

    hops = [(s, h, way) for s in range(4) for h in range(2) for way in (CW, CCW)]
    hops = [m for m in hops if m[0] > 0 or m[1] == m[2]]
    ready = []
    for s, h, way in hops:
        k = 4 - s if way == CW else 4 + s
        if k not in ready:
            from_peer(k)
            ready.append(k)
        value = summand(k, h)
        if (s - 1, h, way) in hops:
            value = value + from_ring(way, s - 1, h)
        ring_out[way, s, h] = value.astype(BF16)
        send(
            ring_out.at[way, s, h],
            ring_in.at[way, s, h],
            rss.at[way, s, h],
            rsr.at[way, s, h],
            (nxt, prv)[way],
            c,
        )

    first_row = 0
    length = 0
    target = 0
    start = 0
    for r in range(span_ref.shape[0]):
        own_it = (owner_ref[r] == d).astype(jnp.int32)
        first_row = first_row + own_it * start
        length = length + own_it * span_ref[r]
        target = target + own_it * offset_ref[r]
        start = start + span_ref[r]
    loads[4].wait()
    cache_rows = dec.shape[0]
    row = lax.broadcasted_iota(jnp.int32, (cache_rows, tokens), 0) - target
    token = lax.broadcasted_iota(jnp.int32, (cache_rows, tokens), 1)
    picks = ((token - first_row) == row) & (row >= 0) & (row < length)
    picked = lax.dot_general(
        picks.astype(F32).astype(BF16), kvt[...], nt, preferred_element_type=F32
    )
    row = lax.broadcasted_iota(jnp.int32, (cache_rows, 1), 0) - target
    written = jnp.where((row >= 0) & (row < length), picked, dec[...].astype(F32))
    cache_ref[...] = written.astype(BF16)

    from_peer(0)
    for h in range(2):
        value = summand(0, h) + from_ring(CW, 3, h) + from_ring(CCW, 3, h)
        for side in range(2):
            columns = slice(side * half + h * quarter, side * half + (h + 1) * quarter)
            out_ref[:, columns] = (
                x_ref[:, columns].astype(F32) + value[8 * side : 8 * side + 8]
            ).astype(BF16)
    for copy in sent:
        copy.wait_send()


def fused_shards(
    stream_in,
    norm_gain,
    w_query,
    w_keyval,
    w_out,
    prefix_cache,
    span_lens,
    prefix_lens,
    owner_dev,
    offsets,
    decode_cache,
):
    chips = lax.axis_size("tensor")
    devices = 2 * chips
    rows, width = stream_in.shape
    tokens = rows * devices
    pre_rows = prefix_cache.shape[0]
    quarter = width // 4
    vmem = pl.BlockSpec(memory_space=pltpu.VMEM)
    smem = pl.BlockSpec(memory_space=pltpu.SMEM)
    hbm = pl.BlockSpec(memory_space=pl.ANY)
    dma = pltpu.SemaphoreType.DMA
    return pl.pallas_call(
        fused,
        out_shape=(
            jax.ShapeDtypeStruct(stream_in.shape, BF16),
            jax.ShapeDtypeStruct(decode_cache.shape, BF16),
        ),
        in_specs=[vmem, vmem] + [smem] * 4 + [hbm] * 5,
        out_specs=(vmem, vmem),
        scratch_shapes=[
            pltpu.VMEM(w_query.shape, BF16),
            pltpu.VMEM(w_keyval.shape, BF16),
            pltpu.VMEM(w_out.shape, BF16),
            pltpu.VMEM(decode_cache.shape, BF16),
            pltpu.VMEM((tokens, width), BF16),
            pltpu.VMEM((8, width // 2), BF16),
            pltpu.VMEM((8, width // 2), BF16),
            pltpu.VMEM((devices * pre_rows, 2 * HEAD), BF16),
            pltpu.VMEM((devices * w_keyval.shape[1], tokens), BF16),
            pltpu.VMEM((tokens, devices * pre_rows), F32),
            pltpu.VMEM((tokens, width), F32),
            pltpu.VMEM((chips, 16, width // 2), BF16),
            pltpu.VMEM((chips, 16, width // 2), BF16),
            pltpu.VMEM((2, 4, 2, 16, quarter), BF16),
            pltpu.VMEM((2, 4, 2, 16, quarter), BF16),
            dma((5,)),
            dma,
            dma,
            dma((2, 4, 2)),
            dma((2, 4, 2)),
            dma((2, 4, 2)),
            dma((2, 4, 2)),
            dma,
            dma,
            dma((4, 2)),
            dma((4, 2)),
            dma((4, 2)),
            dma((4, 2)),
            dma((devices,)),
            dma((devices,)),
            dma((chips,)),
            dma((chips,)),
            dma((2, 4, 2)),
            dma((2, 4, 2)),
        ],
        compiler_params=pltpu.CompilerParams(
            collective_id=0, has_side_effects=True, vmem_limit_bytes=48 * 1024 * 1024
        ),
        name="fused_attention",
    )(
        stream_in,
        norm_gain.reshape(1, width),
        span_lens,
        prefix_lens,
        owner_dev,
        offsets,
        w_query,
        w_keyval,
        w_out,
        prefix_cache,
        decode_cache,
    )


def solution(mesh):
    in_specs = (
        P(("groups", "tensor", "role"), None),
        P(),
        P(None, ("tensor", "role")),
        P(None, ("tensor", "role")),
        P(("tensor", "role"), None),
        P(("groups", "tensor", "role"), None),
        P("groups"),
        P("groups"),
        P("groups"),
        P("groups"),
        P(("groups", "tensor", "role"), None),
    )
    out_specs = (P(("groups", "tensor", "role"), None), P(("groups", "tensor", "role"), None))
    small = mesh.shape["tensor"] == 8 and mesh.shape["role"] == 2
    body = fused_shards if small else shards
    return jax.shard_map(body, mesh=mesh, in_specs=in_specs, out_specs=out_specs, check_vma=False)
```

```python
import jax
import jax.numpy as jnp
from jax import lax
from jax.experimental import pallas as pl
from jax.experimental.pallas import tpu as pltpu
from jax.sharding import PartitionSpec as P

HEAD = 128
GROUP = 8


epsilon = 1e-05
negative = -1e30


def segment_of(positions, lengths):
    run_ends = jnp.cumsum(lengths)
    return jnp.sum((positions[:, None] >= run_ends[None, :]).astype(jnp.int32), axis=1)


def shards(
    stream_in,
    norm_gain,
    w_query,
    w_keyval,
    w_out,
    prefix_cache,
    span_lens,
    prefix_lens,
    owner_dev,
    offsets,
    decode_cache,
):
    devices = lax.axis_size(("tensor", "role"))
    myself = lax.axis_index(("tensor", "role"))
    span_rows = stream_in.shape[0] * devices
    local_pre = prefix_cache.shape[0]
    kv_heads = devices // GROUP
    score_scale = 1.0 / HEAD**0.5
    floats = stream_in.astype(jnp.float32)
    normed = (
        floats
        * lax.rsqrt(jnp.mean(floats * floats, axis=1, keepdims=True) + epsilon)
        * norm_gain.astype(jnp.float32)
    ).astype(jnp.bfloat16)
    shard_rows = lax.all_gather(normed, ("tensor", "role"), axis=0, tiled=True)
    projected = jnp.concatenate(
        [
            jnp.dot(shard_rows, w_query, preferred_element_type=jnp.float32),
            jnp.dot(shard_rows, w_keyval, preferred_element_type=jnp.float32),
        ],
        axis=1,
    )
    queries = projected[:, :HEAD].astype(jnp.bfloat16)
    kv_local = projected[:, HEAD:].astype(jnp.bfloat16)
    keyval = lax.all_gather(kv_local, ("tensor", "role"), axis=1, tiled=True)
    column_base = myself // GROUP * (2 * HEAD)
    span_keys = lax.dynamic_slice_in_dim(keyval, column_base, HEAD, 1)
    span_values = lax.dynamic_slice_in_dim(keyval, column_base + HEAD, HEAD, 1)
    row_index = jnp.arange(span_rows, dtype=jnp.int32)
    tok_seg = segment_of(row_index, span_lens)
    span_mask = (tok_seg[:, None] == tok_seg[None, :]) & (row_index[:, None] >= row_index[None, :])
    span_scores = jnp.where(
        span_mask,
        jnp.dot(queries, span_keys.T, preferred_element_type=jnp.float32) * score_scale,
        negative,
    )
    stored = jnp.transpose(prefix_cache.reshape(local_pre, kv_heads, 2 * HEAD), (1, 0, 2))
    span_max = jnp.max(span_scores, axis=1)
    span_weights = jnp.where(span_mask, jnp.exp(span_scores - span_max[:, None]), 0.0)
    start_carry = (
        span_max,
        jnp.sum(span_weights, axis=1),
        jnp.dot(span_weights.astype(jnp.bfloat16), span_values, preferred_element_type=jnp.float32),
    )
    repeated = jnp.repeat(stored, GROUP, axis=0)
    received = lax.all_to_all(repeated, ("tensor", "role"), split_axis=0, concat_axis=1, tiled=True)
    all_rows = devices * local_pre
    factor_count = 1
    while devices % (factor_count * 2) == 0 and factor_count * 2 * local_pre <= 512:
        factor_count = factor_count * 2
    block_rows = factor_count * local_pre
    blocks = received.reshape(all_rows // block_rows, block_rows, 2 * HEAD)

    def absorb(running, block_pair):
        row_max, row_total, summed = running
        block_number, shard_rows = block_pair
        row_start = block_number * block_rows
        key_seg = segment_of(row_start + jnp.arange(block_rows, dtype=jnp.int32), prefix_lens)
        visible = tok_seg[:, None] == key_seg[None, :]
        key_rows = shard_rows[:, :HEAD]
        value_rows = shard_rows[:, HEAD:]
        scores = jnp.where(
            visible,
            jnp.dot(queries, key_rows.T, preferred_element_type=jnp.float32) * score_scale,
            negative,
        )
        new_max = jnp.maximum(row_max, jnp.max(scores, axis=1))
        factor = jnp.exp(row_max - new_max)
        weights = jnp.where(visible, jnp.exp(scores - new_max[:, None]), 0.0)
        summed = summed * factor[:, None] + jnp.dot(
            weights.astype(jnp.bfloat16), value_rows, preferred_element_type=jnp.float32
        )
        return ((new_max, row_total * factor + jnp.sum(weights, axis=1), summed), None)

    numbers = jnp.arange(all_rows // block_rows, dtype=jnp.int32)
    (row_max, row_total, summed), unused = lax.scan(absorb, start_carry, (numbers, blocks))
    attention = (summed / row_total[:, None]).astype(jnp.bfloat16)
    stream_out = (
        floats
        + lax.psum_scatter(
            jnp.dot(attention, w_out, preferred_element_type=jnp.float32),
            ("tensor", "role"),
            scatter_dimension=0,
            tiled=True,
        )
    ).astype(jnp.bfloat16)
    owned = owner_dev == myself
    owned_count = jnp.sum(owned.astype(jnp.int32))
    starts = jnp.cumsum(span_lens) - span_lens
    first_row = jnp.sum(jnp.where(owned, starts, 0))
    length = jnp.sum(jnp.where(owned, span_lens, 0))
    target = jnp.sum(jnp.where(owned, offsets, 0))
    padded = jnp.concatenate(
        [keyval, jnp.zeros((span_rows, keyval.shape[1]), jnp.bfloat16)], axis=0
    )
    kv_block = lax.dynamic_slice_in_dim(padded, first_row, span_rows, 0)
    before = lax.dynamic_slice_in_dim(decode_cache, target, span_rows, 0)
    keep_new = (row_index < length) & (owned_count > 0)
    written = jnp.where(keep_new[:, None], kv_block, before)
    cache_out = lax.dynamic_update_slice_in_dim(decode_cache, written, target, 0)
    return (stream_out, cache_out)


MESH = pl.DeviceIdType.MESH
F32 = jnp.float32
BF16 = jnp.bfloat16
CW, CCW = 0, 1


def chip_at(position, chips):
    back = position // (chips // 2)
    return (1 - back) * 2 * position + back * (2 * (chips - 1 - position) + 1)


def fused(
    x_ref,
    gain_ref,
    span_ref,
    plen_ref,
    owner_ref,
    offset_ref,
    wq_hbm,
    wkv_hbm,
    wout_hbm,
    pre_hbm,
    dec_hbm,
    out_ref,
    cache_ref,
    wq,
    wkv,
    wout,
    dec,
    normed,
    xsend,
    xrecv,
    kvbuf,
    kvt,
    qall,
    sums_out,
    sums_in,
    scores,
    part,
    peer_out,
    peer_in,
    ring_out,
    ring_in,
    lsem,
    xs,
    xr,
    ags,
    agr,
    pfs,
    pfr,
    p1s,
    p1r,
    p2s,
    p2r,
    pps,
    ppr,
    kvs,
    kvr,
    qs,
    qr,
    ss,
    sr,
    pes,
    per,
    rss,
    rsr,
):
    chips = lax.axis_size("tensor")
    devices = 2 * chips
    t = lax.axis_index("tensor")
    c = lax.axis_index("role")
    peer = 1 - c
    d = 2 * t + c
    odd = t % 2
    pos = (1 - odd) * (t // 2) + odd * (chips - 1 - t // 2)
    nxt = chip_at((pos + 1) % chips, chips)
    prv = chip_at((pos + chips - 1) % chips, chips)
    width = x_ref.shape[1]
    half = width // 2
    quarter = width // 4
    tokens = 16 * chips
    pre_rows = pre_hbm.shape[0]
    g = t // 4
    y = t % 2
    across = t + 1 - 2 * y
    along = t + 2 - 4 * ((t // 2) % 2)

    def remote(src, dst, ssem, rsem, tt, cc):
        return pltpu.make_async_remote_copy(
            src_ref=src,
            dst_ref=dst,
            send_sem=ssem,
            recv_sem=rsem,
            device_id={"tensor": tt, "role": cc},
            device_id_type=MESH,
        )

    sent = []

    def send(*args):
        copy = remote(*args)
        copy.start()
        sent.append(copy)

    barrier = pltpu.get_barrier_semaphore()
    for r in range(1, devices):
        other = (d + r) % devices
        pl.semaphore_signal(
            barrier, inc=1, device_id={"tensor": other // 2, "role": other % 2}, device_id_type=MESH
        )

    def pre_slot(which, row, core):
        index = which * 4 + row * 2 + core
        return kvbuf.at[pl.ds(pl.multiple_of(index * pre_rows, pre_rows), pre_rows), :]

    def head_columns(head):
        return pre_hbm.at[:, pl.ds(pl.multiple_of(head * 2 * HEAD, 2 * HEAD), 2 * HEAD)]

    loads = [
        pltpu.make_async_copy(head_columns(g), pre_slot(0, y, c), lsem.at[0]),
        pltpu.make_async_copy(wkv_hbm, wkv, lsem.at[1]),
        pltpu.make_async_copy(wq_hbm, wq, lsem.at[2]),
        pltpu.make_async_copy(wout_hbm, wout, lsem.at[3]),
        pltpu.make_async_copy(dec_hbm, dec, lsem.at[4]),
    ]
    for load in loads:
        load.start()

    floats = x_ref[...].astype(F32)
    mine = floats * lax.rsqrt(jnp.mean(floats * floats, axis=1, keepdims=True) + epsilon)
    mine = mine * gain_ref[...].astype(F32).reshape(1, width)
    is_one = (c == 1).astype(F32)
    left, right = mine[:, :half], mine[:, half:]
    xsend[...] = jnp.where(is_one > 0.5, left, right).astype(BF16)
    kept = jnp.where(is_one > 0.5, right, left).astype(BF16).astype(F32)

    pl.semaphore_wait(barrier, devices - 1)
    send(xsend, xrecv, xs, xr, t, peer)

    def block(chip, core, h=None):
        column = core * half if h is None else core * half + h * quarter
        size = half if h is None else quarter
        return (
            pl.ds(pl.multiple_of(16 * chip, 16), 16),
            pl.ds(pl.multiple_of(column, quarter), size),
        )

    remote(xsend, xrecv, xs, xr, t, peer).wait_recv()
    theirs = xrecv[...].astype(F32)
    first = jnp.where(is_one > 0.5, theirs, kept)
    second = jnp.where(is_one > 0.5, kept, theirs)
    normed[block(t, c)] = jnp.concatenate([first, second], axis=0).astype(BF16)

    def source(way, hops):
        return chip_at((pos + chips - hops) % chips if way == CW else (pos + hops) % chips, chips)

    def hop(way, s, h):
        here = normed.at[block(source(way, s), c, h)]
        send(here, here, ags.at[way, s, h], agr.at[way, s, h], (nxt, prv)[way], c)

    last = chips // 2 - 1
    own = normed.at[block(t, c)]
    messages = [(s, h, way) for s in range(last + 1) for h in range(2) for way in (CW, CCW)]
    messages = [m for m in messages if m[0] < last or m[1] == m[2]]
    for s, h, way in messages:
        if s == 0:
            hop(way, 0, h)
    send(own, own, pfs.at[0, last, 1], pfr.at[0, last, 1], t, peer)
    for s, h, way in messages:
        landed = normed.at[block(source(way, s + 1), c, h)]
        remote(landed, landed, ags.at[way, s, h], agr.at[way, s, h], nxt, c).wait_recv()
        if (s + 1, h, way) in messages:
            hop(way, s + 1, h)
        send(landed, landed, pfs.at[way, s, h], pfr.at[way, s, h], t, peer)

    loads[0].wait()
    send(head_columns(1 - g), pre_slot(1, y, c), p1s, p1r, (t + 4) % chips, c)

    def spread(which):
        slot = pre_slot(which, y, c)
        send(slot, slot, p2s.at[which], p2r.at[which], across, c)
        send(slot, slot, pps.at[which, 0], ppr.at[which, 0], t, peer)

    spread(0)

    own = normed.at[block(t, peer)]
    remote(own, own, pfs.at[0, last, 1], pfr.at[0, last, 1], t, peer).wait_recv()
    for s, h, way in messages:
        landed = normed.at[block(source(way, s + 1), peer, h)]
        remote(landed, landed, pfs.at[way, s, h], pfr.at[way, s, h], t, peer).wait_recv()
    loads[1].wait()
    nt = (((1,), (1,)), ((), ()))
    kv = lax.dot_general(wkv[...], normed[...], nt, preferred_element_type=F32)
    kv_rows = wkv.shape[0]

    def kv_slot(index):
        return kvt.at[pl.ds(pl.multiple_of(index * kv_rows, kv_rows), kv_rows), :]

    kv_slot(d)[...] = kv.astype(BF16)
    for r in range(1, devices):
        other = (d + r) % devices
        send(kv_slot(d), kv_slot(d), kvs.at[r], kvr.at[r], other // 2, other % 2)
    loads[2].wait()
    queries = jnp.dot(normed[...], wq[...], preferred_element_type=F32).astype(BF16)
    qall[:tokens, :] = queries
    send(qall.at[pl.ds(0, tokens)], qall.at[pl.ds(tokens, tokens)], qs, qr, along, c)
    slot = pre_slot(1, y, c)
    remote(slot, slot, p1s, p1r, t, peer).wait_recv()
    spread(1)

    def segments(positions, ref):
        end = 0
        total = jnp.zeros_like(positions)
        for r in range(ref.shape[0]):
            end = end + ref[r]
            total = total + (positions >= end).astype(jnp.int32)
        return total

    tok_col = segments(lax.broadcasted_iota(jnp.int32, (tokens, 1), 0), span_ref)
    tok_row = segments(lax.broadcasted_iota(jnp.int32, (1, tokens), 1), span_ref)

    def wait_slot(slot, ssem, rsem):
        remote(slot, slot, ssem, rsem, t, peer).wait_recv()

    score_scale = 1.0 / HEAD**0.5
    tok_two = jnp.concatenate([tok_col, tok_col], axis=0)
    tile = 2 * pre_rows
    seen = []
    tops = None
    wait_slot(pre_slot(0, 1 - y, c), p2s.at[0], p2r.at[0])
    send(pre_slot(0, 1 - y, c), pre_slot(0, 1 - y, c), pps.at[0, 1], ppr.at[0, 1], t, peer)
    remote(
        qall.at[pl.ds(0, tokens)], qall.at[pl.ds(tokens, tokens)], qs, qr, t, peer
    ).wait_recv()
    pieces = [(0, 0), (0, 1), (1, 0), (1, 1)]

    def piece_rows(which, rel):
        chip_row = y if rel == 0 else 1 - y
        return pl.ds(pl.multiple_of((which * 2 + chip_row) * tile, tile), tile)

    for i, (which, rel) in enumerate(pieces):
        chip_row = y if rel == 0 else 1 - y
        if (which, rel) == (1, 1):
            wait_slot(pre_slot(1, chip_row, c), p2s.at[1], p2r.at[1])
            slot = pre_slot(1, chip_row, c)
            send(slot, slot, pps.at[1, 1], ppr.at[1, 1], t, peer)
        wait_slot(pre_slot(which, chip_row, peer), pps.at[which, rel], ppr.at[which, rel])
        chip = (2 * (t // 2) + 4 * which) % chips + chip_row
        seg = segments(lax.broadcasted_iota(jnp.int32, (1, tile), 1) + chip * tile, plen_ref)
        seen.append(seg)
        raw = lax.dot_general(
            qall[...], kvbuf[piece_rows(which, rel), :HEAD], nt, preferred_element_type=F32
        )
        masked = jnp.where(tok_two == seg, raw * score_scale, negative)
        scores[:, i * tile : (i + 1) * tile] = masked
        top = jnp.max(masked, axis=1, keepdims=True)
        tops = top if tops is None else jnp.maximum(tops, top)

    def absorb(first_row):
        rows = slice(first_row, first_row + tokens)
        top = tops[rows]
        total = jnp.zeros((tokens, 1), F32)
        product = jnp.zeros((tokens, HEAD), F32)
        for i, (which, rel) in enumerate(pieces):
            weights = jnp.exp(scores[rows, i * tile : (i + 1) * tile] - top)
            weights = jnp.where(tok_col == seen[i], weights, 0.0)
            total = total + jnp.sum(weights, axis=1, keepdims=True)
            product = product + jnp.dot(
                weights.astype(BF16), kvbuf[piece_rows(which, rel), HEAD:], preferred_element_type=F32
            )
        return top, total, product

    top, total, product = absorb(tokens)
    lane = lax.broadcasted_iota(jnp.int32, (tokens, tokens), 1)
    turned = jnp.transpose(jnp.where(lane < tokens // 2, top, total))
    sums_out[:tokens, :] = product
    sums_out[tokens:, :] = turned[tokens // 2 - 8 : tokens // 2 + 8]
    send(sums_out, sums_in, ss, sr, along, c)
    top, total, product = absorb(0)

    for r in range(1, devices):
        slot = kv_slot((d + devices - r) % devices)
        remote(slot, slot, kvs.at[r], kvr.at[r], t, peer).wait_recv()
    key_base = pl.multiple_of(g * 2 * HEAD, 2 * HEAD)
    span_keys = kvt[pl.ds(key_base, HEAD), :]
    span_values = kvt[pl.ds(key_base + HEAD, HEAD), :]
    before = lax.broadcasted_iota(jnp.int32, (tokens, tokens), 0) >= lax.broadcasted_iota(
        jnp.int32, (tokens, tokens), 1
    )
    span_mask = (tok_col == tok_row) & before
    span_scores = jnp.where(
        span_mask, jnp.dot(queries, span_keys, preferred_element_type=F32) * score_scale, negative
    )
    remote(sums_out, sums_in, ss, sr, t, peer).wait_recv()
    turned = jnp.transpose(jnp.concatenate([sums_in[tokens:, :]] * (tokens // 16), axis=0))
    other_top, other_total = turned[:, 0:1], turned[:, 8:9]
    span_top = jnp.max(span_scores, axis=1, keepdims=True)
    row_max = jnp.maximum(jnp.maximum(top, other_top), span_top)
    weights = jnp.where(span_mask, jnp.exp(span_scores - row_max), 0.0)
    factor, other_factor = jnp.exp(top - row_max), jnp.exp(other_top - row_max)
    row_total = (
        jnp.sum(weights, axis=1, keepdims=True) + total * factor + other_total * other_factor
    )
    summed = lax.dot_general(weights.astype(BF16), span_values, nt, preferred_element_type=F32)
    summed = summed + product * factor + sums_in[:tokens, :] * other_factor
    attention = (summed / row_total).astype(BF16)

    loads[3].wait()
    step = 1024
    for i in range(width // step):
        part[:, i * step : (i + 1) * step] = jnp.dot(
            attention, wout[:, i * step : (i + 1) * step], preferred_element_type=F32
        )

    def stacked(k, core, h):
        rows = pl.ds(pl.multiple_of(16 * chip_at((pos + k) % chips, chips) + 8 * core, 8), 8)
        top = part[rows, h * quarter : (h + 1) * quarter]
        bottom = part[rows, half + h * quarter : half + (h + 1) * quarter]
        return jnp.concatenate([top, bottom], axis=0)

    order = [4, 3, 5, 2, 6, 1, 7, 0]
    for k in order:
        for h in range(2):
            peer_out[k, :, h * quarter : (h + 1) * quarter] = stacked(k, peer, h).astype(BF16)
        send(peer_out.at[k], peer_in.at[k], pes.at[k], per.at[k], t, peer)

    def summand(k, h):
        return stacked(k, c, h) + peer_in[k, :, h * quarter : (h + 1) * quarter].astype(F32)

    def from_peer(k):
        remote(peer_out.at[k], peer_in.at[k], pes.at[k], per.at[k], t, peer).wait_recv()

    def from_ring(way, s, h):
        remote(
            ring_out.at[way, s, h], ring_in.at[way, s, h], rss.at[way, s, h], rsr.at[way, s, h], nxt, c
        ).wait_recv()
        return ring_in[way, s, h].astype(F32)

    hops = [(s, h, way) for s in range(4) for h in range(2) for way in (CW, CCW)]
    hops = [m for m in hops if m[0] > 0 or m[1] == m[2]]
    ready = []
    for s, h, way in hops:
        k = 4 - s if way == CW else 4 + s
        if k not in ready:
            from_peer(k)
            ready.append(k)
        value = summand(k, h)
        if (s - 1, h, way) in hops:
            value = value + from_ring(way, s - 1, h)
        ring_out[way, s, h] = value.astype(BF16)
        send(
            ring_out.at[way, s, h],
            ring_in.at[way, s, h],
            rss.at[way, s, h],
            rsr.at[way, s, h],
            (nxt, prv)[way],
            c,
        )

    first_row = 0
    length = 0
    target = 0
    start = 0
    for r in range(span_ref.shape[0]):
        own_it = (owner_ref[r] == d).astype(jnp.int32)
        first_row = first_row + own_it * start
        length = length + own_it * span_ref[r]
        target = target + own_it * offset_ref[r]
        start = start + span_ref[r]
    loads[4].wait()
    cache_rows = dec.shape[0]
    row = lax.broadcasted_iota(jnp.int32, (cache_rows, tokens), 0) - target
    token = lax.broadcasted_iota(jnp.int32, (cache_rows, tokens), 1)
    picks = ((token - first_row) == row) & (row >= 0) & (row < length)
    picked = lax.dot_general(
        picks.astype(F32).astype(BF16), kvt[...], nt, preferred_element_type=F32
    )
    row = lax.broadcasted_iota(jnp.int32, (cache_rows, 1), 0) - target
    written = jnp.where((row >= 0) & (row < length), picked, dec[...].astype(F32))
    cache_ref[...] = written.astype(BF16)

    from_peer(0)
    for h in range(2):
        value = summand(0, h) + from_ring(CW, 3, h) + from_ring(CCW, 3, h)
        for side in range(2):
            columns = slice(side * half + h * quarter, side * half + (h + 1) * quarter)
            out_ref[:, columns] = (
                x_ref[:, columns].astype(F32) + value[8 * side : 8 * side + 8]
            ).astype(BF16)
    for copy in sent:
        copy.wait_send()


def fused_shards(
    stream_in,
    norm_gain,
    w_query,
    w_keyval,
    w_out,
    prefix_cache,
    span_lens,
    prefix_lens,
    owner_dev,
    offsets,
    decode_cache,
):
    chips = lax.axis_size("tensor")
    devices = 2 * chips
    rows, width = stream_in.shape
    tokens = rows * devices
    pre_rows = prefix_cache.shape[0]
    quarter = width // 4
    vmem = pl.BlockSpec(memory_space=pltpu.VMEM)
    smem = pl.BlockSpec(memory_space=pltpu.SMEM)
    hbm = pl.BlockSpec(memory_space=pl.ANY)
    dma = pltpu.SemaphoreType.DMA
    return pl.pallas_call(
        fused,
        out_shape=(
            jax.ShapeDtypeStruct(stream_in.shape, BF16),
            jax.ShapeDtypeStruct(decode_cache.shape, BF16),
        ),
        in_specs=[vmem, vmem] + [smem] * 4 + [hbm] * 5,
        out_specs=(vmem, vmem),
        scratch_shapes=[
            pltpu.VMEM(w_query.shape, BF16),
            pltpu.VMEM((w_keyval.shape[1], width), BF16),
            pltpu.VMEM(w_out.shape, BF16),
            pltpu.VMEM(decode_cache.shape, BF16),
            pltpu.VMEM((tokens, width), BF16),
            pltpu.VMEM((8, width // 2), BF16),
            pltpu.VMEM((8, width // 2), BF16),
            pltpu.VMEM((devices // 2 * pre_rows, 2 * HEAD), BF16),
            pltpu.VMEM((devices * w_keyval.shape[1], tokens), BF16),
            pltpu.VMEM((2 * tokens, HEAD), BF16),
            pltpu.VMEM((tokens + 16, HEAD), F32),
            pltpu.VMEM((tokens + 16, HEAD), F32),
            pltpu.VMEM((2 * tokens, devices // 2 * pre_rows), F32),
            pltpu.VMEM((tokens, width), F32),
            pltpu.VMEM((chips, 16, width // 2), BF16),
            pltpu.VMEM((chips, 16, width // 2), BF16),
            pltpu.VMEM((2, 4, 2, 16, quarter), BF16),
            pltpu.VMEM((2, 4, 2, 16, quarter), BF16),
            dma((5,)),
            dma,
            dma,
            dma((2, 4, 2)),
            dma((2, 4, 2)),
            dma((2, 4, 2)),
            dma((2, 4, 2)),
            dma,
            dma,
            dma((2,)),
            dma((2,)),
            dma((2, 2)),
            dma((2, 2)),
            dma((devices,)),
            dma((devices,)),
            dma,
            dma,
            dma,
            dma,
            dma((chips,)),
            dma((chips,)),
            dma((2, 4, 2)),
            dma((2, 4, 2)),
        ],
        compiler_params=pltpu.CompilerParams(
            collective_id=0, has_side_effects=True, vmem_limit_bytes=60 * 1024 * 1024
        ),
        name="fused_attention",
    )(
        stream_in,
        norm_gain,
        span_lens,
        prefix_lens,
        owner_dev,
        offsets,
        w_query,
        w_keyval.T,
        w_out,
        prefix_cache,
        decode_cache,
    )


def solution(mesh):
    in_specs = (
        P(("groups", "tensor", "role"), None),
        P(),
        P(None, ("tensor", "role")),
        P(None, ("tensor", "role")),
        P(("tensor", "role"), None),
        P(("groups", "tensor", "role"), None),
        P("groups"),
        P("groups"),
        P("groups"),
        P("groups"),
        P(("groups", "tensor", "role"), None),
    )
    out_specs = (P(("groups", "tensor", "role"), None), P(("groups", "tensor", "role"), None))
    small = mesh.shape["tensor"] == 8 and mesh.shape["role"] == 2
    body = fused_shards if small else shards
    return jax.shard_map(body, mesh=mesh, in_specs=in_specs, out_specs=out_specs, check_vma=False)
```

```python
import jax
import jax.numpy as jnp
from jax import lax
from jax.experimental import pallas as pl
from jax.experimental.pallas import tpu as pltpu
from jax.sharding import PartitionSpec as P

HEAD = 128
GROUP = 8


epsilon = 1e-05
negative = -1e30


def segment_of(positions, lengths):
    run_ends = jnp.cumsum(lengths)
    return jnp.sum((positions[:, None] >= run_ends[None, :]).astype(jnp.int32), axis=1)


def shards(
    stream_in,
    norm_gain,
    w_query,
    w_keyval,
    w_out,
    prefix_cache,
    span_lens,
    prefix_lens,
    owner_dev,
    offsets,
    decode_cache,
):
    devices = lax.axis_size(("tensor", "role"))
    myself = lax.axis_index(("tensor", "role"))
    span_rows = stream_in.shape[0] * devices
    local_pre = prefix_cache.shape[0]
    kv_heads = devices // GROUP
    score_scale = 1.0 / HEAD**0.5
    floats = stream_in.astype(jnp.float32)
    normed = (
        floats
        * lax.rsqrt(jnp.mean(floats * floats, axis=1, keepdims=True) + epsilon)
        * norm_gain.astype(jnp.float32)
    ).astype(jnp.bfloat16)
    shard_rows = lax.all_gather(normed, ("tensor", "role"), axis=0, tiled=True)
    projected = jnp.concatenate(
        [
            jnp.dot(shard_rows, w_query, preferred_element_type=jnp.float32),
            jnp.dot(shard_rows, w_keyval, preferred_element_type=jnp.float32),
        ],
        axis=1,
    )
    queries = projected[:, :HEAD].astype(jnp.bfloat16)
    kv_local = projected[:, HEAD:].astype(jnp.bfloat16)
    keyval = lax.all_gather(kv_local, ("tensor", "role"), axis=1, tiled=True)
    column_base = myself // GROUP * (2 * HEAD)
    span_keys = lax.dynamic_slice_in_dim(keyval, column_base, HEAD, 1)
    span_values = lax.dynamic_slice_in_dim(keyval, column_base + HEAD, HEAD, 1)
    row_index = jnp.arange(span_rows, dtype=jnp.int32)
    tok_seg = segment_of(row_index, span_lens)
    span_mask = (tok_seg[:, None] == tok_seg[None, :]) & (row_index[:, None] >= row_index[None, :])
    span_scores = jnp.where(
        span_mask,
        jnp.dot(queries, span_keys.T, preferred_element_type=jnp.float32) * score_scale,
        negative,
    )
    stored = jnp.transpose(prefix_cache.reshape(local_pre, kv_heads, 2 * HEAD), (1, 0, 2))
    span_max = jnp.max(span_scores, axis=1)
    span_weights = jnp.where(span_mask, jnp.exp(span_scores - span_max[:, None]), 0.0)
    start_carry = (
        span_max,
        jnp.sum(span_weights, axis=1),
        jnp.dot(span_weights.astype(jnp.bfloat16), span_values, preferred_element_type=jnp.float32),
    )
    repeated = jnp.repeat(stored, GROUP, axis=0)
    received = lax.all_to_all(repeated, ("tensor", "role"), split_axis=0, concat_axis=1, tiled=True)
    all_rows = devices * local_pre
    factor_count = 1
    while devices % (factor_count * 2) == 0 and factor_count * 2 * local_pre <= 512:
        factor_count = factor_count * 2
    block_rows = factor_count * local_pre
    blocks = received.reshape(all_rows // block_rows, block_rows, 2 * HEAD)

    def absorb(running, block_pair):
        row_max, row_total, summed = running
        block_number, shard_rows = block_pair
        row_start = block_number * block_rows
        key_seg = segment_of(row_start + jnp.arange(block_rows, dtype=jnp.int32), prefix_lens)
        visible = tok_seg[:, None] == key_seg[None, :]
        key_rows = shard_rows[:, :HEAD]
        value_rows = shard_rows[:, HEAD:]
        scores = jnp.where(
            visible,
            jnp.dot(queries, key_rows.T, preferred_element_type=jnp.float32) * score_scale,
            negative,
        )
        new_max = jnp.maximum(row_max, jnp.max(scores, axis=1))
        factor = jnp.exp(row_max - new_max)
        weights = jnp.where(visible, jnp.exp(scores - new_max[:, None]), 0.0)
        summed = summed * factor[:, None] + jnp.dot(
            weights.astype(jnp.bfloat16), value_rows, preferred_element_type=jnp.float32
        )
        return ((new_max, row_total * factor + jnp.sum(weights, axis=1), summed), None)

    numbers = jnp.arange(all_rows // block_rows, dtype=jnp.int32)
    (row_max, row_total, summed), unused = lax.scan(absorb, start_carry, (numbers, blocks))
    attention = (summed / row_total[:, None]).astype(jnp.bfloat16)
    stream_out = (
        floats
        + lax.psum_scatter(
            jnp.dot(attention, w_out, preferred_element_type=jnp.float32),
            ("tensor", "role"),
            scatter_dimension=0,
            tiled=True,
        )
    ).astype(jnp.bfloat16)
    owned = owner_dev == myself
    owned_count = jnp.sum(owned.astype(jnp.int32))
    starts = jnp.cumsum(span_lens) - span_lens
    first_row = jnp.sum(jnp.where(owned, starts, 0))
    length = jnp.sum(jnp.where(owned, span_lens, 0))
    target = jnp.sum(jnp.where(owned, offsets, 0))
    padded = jnp.concatenate(
        [keyval, jnp.zeros((span_rows, keyval.shape[1]), jnp.bfloat16)], axis=0
    )
    kv_block = lax.dynamic_slice_in_dim(padded, first_row, span_rows, 0)
    before = lax.dynamic_slice_in_dim(decode_cache, target, span_rows, 0)
    keep_new = (row_index < length) & (owned_count > 0)
    written = jnp.where(keep_new[:, None], kv_block, before)
    cache_out = lax.dynamic_update_slice_in_dim(decode_cache, written, target, 0)
    return (stream_out, cache_out)


MESH = pl.DeviceIdType.MESH
F32 = jnp.float32
BF16 = jnp.bfloat16
CW, CCW = 0, 1


def chip_at(position, chips):
    back = position // (chips // 2)
    return (1 - back) * 2 * position + back * (2 * (chips - 1 - position) + 1)


def fused(
    x_ref,
    gain_ref,
    span_ref,
    plen_ref,
    owner_ref,
    offset_ref,
    wq_hbm,
    wkv_hbm,
    wout_hbm,
    pre_hbm,
    dec_hbm,
    out_ref,
    cache_ref,
    wq,
    wkv,
    wout,
    dec,
    normed,
    xsend,
    xrecv,
    kvbuf,
    kvt,
    qall,
    sums_out,
    sums_in,
    scores,
    part,
    peer_out,
    peer_in,
    ring_out,
    ring_in,
    lsem,
    xs,
    xr,
    ags,
    agr,
    pfs,
    pfr,
    p1s,
    p1r,
    p2s,
    p2r,
    pps,
    ppr,
    kvs,
    kvr,
    qs,
    qr,
    ss,
    sr,
    pes,
    per,
    rss,
    rsr,
):
    chips = lax.axis_size("tensor")
    devices = 2 * chips
    t = lax.axis_index("tensor")
    c = lax.axis_index("role")
    peer = 1 - c
    d = 2 * t + c
    odd = t % 2
    pos = (1 - odd) * (t // 2) + odd * (chips - 1 - t // 2)
    nxt = chip_at((pos + 1) % chips, chips)
    prv = chip_at((pos + chips - 1) % chips, chips)
    width = x_ref.shape[1]
    half = width // 2
    quarter = width // 4
    tokens = 16 * chips
    pre_rows = pre_hbm.shape[0]
    g = t // 4
    y = t % 2
    across = t + 1 - 2 * y
    along = t + 2 - 4 * ((t // 2) % 2)

    def remote(src, dst, ssem, rsem, tt, cc):
        return pltpu.make_async_remote_copy(
            src_ref=src,
            dst_ref=dst,
            send_sem=ssem,
            recv_sem=rsem,
            device_id={"tensor": tt, "role": cc},
            device_id_type=MESH,
        )

    sent = []

    def send(*args):
        copy = remote(*args)
        copy.start()
        sent.append(copy)

    barrier = pltpu.get_barrier_semaphore()
    for r in range(1, devices):
        other = (d + r) % devices
        pl.semaphore_signal(
            barrier, inc=1, device_id={"tensor": other // 2, "role": other % 2}, device_id_type=MESH
        )

    def pre_slot(which, row, core):
        index = which * 4 + row * 2 + core
        return kvbuf.at[pl.ds(pl.multiple_of(index * pre_rows, pre_rows), pre_rows), :]

    def head_columns(head):
        return pre_hbm.at[:, pl.ds(pl.multiple_of(head * 2 * HEAD, 2 * HEAD), 2 * HEAD)]

    loads = [
        pltpu.make_async_copy(head_columns(g), pre_slot(0, y, c), lsem.at[0]),
        pltpu.make_async_copy(wkv_hbm, wkv, lsem.at[1]),
        pltpu.make_async_copy(wq_hbm, wq, lsem.at[2]),
        pltpu.make_async_copy(wout_hbm, wout, lsem.at[3]),
        pltpu.make_async_copy(dec_hbm, dec, lsem.at[4]),
    ]
    for load in loads:
        load.start()

    floats = x_ref[...].astype(F32)
    mine = floats * lax.rsqrt(jnp.mean(floats * floats, axis=1, keepdims=True) + epsilon)
    mine = mine * gain_ref[...].astype(F32).reshape(1, width)
    is_one = (c == 1).astype(F32)
    left, right = mine[:, :half], mine[:, half:]
    xsend[...] = jnp.where(is_one > 0.5, left, right).astype(BF16)
    kept = jnp.where(is_one > 0.5, right, left).astype(BF16).astype(F32)

    pl.semaphore_wait(barrier, devices - 1)
    send(xsend, xrecv, xs, xr, t, peer)

    def block(chip, core, h=None):
        column = core * half if h is None else core * half + h * quarter
        size = half if h is None else quarter
        return (
            pl.ds(pl.multiple_of(16 * chip, 16), 16),
            pl.ds(pl.multiple_of(column, quarter), size),
        )

    remote(xsend, xrecv, xs, xr, t, peer).wait_recv()
    theirs = xrecv[...].astype(F32)
    first = jnp.where(is_one > 0.5, theirs, kept)
    second = jnp.where(is_one > 0.5, kept, theirs)
    normed[block(t, c)] = jnp.concatenate([first, second], axis=0).astype(BF16)

    def source(way, hops):
        return chip_at((pos + chips - hops) % chips if way == CW else (pos + hops) % chips, chips)

    def hop(way, s, h):
        here = normed.at[block(source(way, s), c, h)]
        send(here, here, ags.at[way, s, h], agr.at[way, s, h], (nxt, prv)[way], c)

    last = chips // 2 - 1
    own = normed.at[block(t, c)]
    messages = [(s, h, way) for s in range(last + 1) for h in range(2) for way in (CW, CCW)]
    messages = [m for m in messages if m[0] < last or m[1] == m[2]]
    messages = sorted(messages, key=lambda m: (m[0], m[1] != m[2]))
    for s, h, way in messages:
        if s == 0:
            hop(way, 0, h)
    send(own, own, pfs.at[0, last, 1], pfr.at[0, last, 1], t, peer)
    for s, h, way in messages:
        landed = normed.at[block(source(way, s + 1), c, h)]
        remote(landed, landed, ags.at[way, s, h], agr.at[way, s, h], nxt, c).wait_recv()
        if (s + 1, h, way) in messages:
            hop(way, s + 1, h)
        send(landed, landed, pfs.at[way, s, h], pfr.at[way, s, h], t, peer)
        if (s, h, way) == (last - 1, 0, CCW):
            send(head_columns(1 - g), pre_slot(1, y, c), p1s, p1r, (t + 4) % chips, c)

    loads[0].wait()

    def spread(which):
        slot = pre_slot(which, y, c)
        send(slot, slot, p2s.at[which], p2r.at[which], across, c)
        send(slot, slot, pps.at[which, 0], ppr.at[which, 0], t, peer)

    spread(0)

    own = normed.at[block(t, peer)]
    remote(own, own, pfs.at[0, last, 1], pfr.at[0, last, 1], t, peer).wait_recv()
    for s, h, way in messages:
        landed = normed.at[block(source(way, s + 1), peer, h)]
        remote(landed, landed, pfs.at[way, s, h], pfr.at[way, s, h], t, peer).wait_recv()
    loads[1].wait()
    nt = (((1,), (1,)), ((), ()))
    kv = lax.dot_general(wkv[...], normed[...], nt, preferred_element_type=F32)
    kv_rows = wkv.shape[0]

    def kv_slot(index):
        return kvt.at[pl.ds(pl.multiple_of(index * kv_rows, kv_rows), kv_rows), :]

    kv_slot(d)[...] = kv.astype(BF16)
    for r in range(1, devices):
        other = (d + r) % devices
        send(kv_slot(d), kv_slot(d), kvs.at[r], kvr.at[r], other // 2, other % 2)
    loads[2].wait()
    queries = jnp.dot(normed[...], wq[...], preferred_element_type=F32).astype(BF16)
    qall[:tokens, :] = queries
    send(qall.at[pl.ds(0, tokens)], qall.at[pl.ds(tokens, tokens)], qs, qr, along, c)
    slot = pre_slot(1, y, c)
    remote(slot, slot, p1s, p1r, t, peer).wait_recv()
    spread(1)

    def segments(positions, ref):
        end = 0
        total = jnp.zeros_like(positions)
        for r in range(ref.shape[0]):
            end = end + ref[r]
            total = total + (positions >= end).astype(jnp.int32)
        return total

    tok_col = segments(lax.broadcasted_iota(jnp.int32, (tokens, 1), 0), span_ref)
    tok_row = segments(lax.broadcasted_iota(jnp.int32, (1, tokens), 1), span_ref)

    def wait_slot(slot, ssem, rsem):
        remote(slot, slot, ssem, rsem, t, peer).wait_recv()

    score_scale = 1.0 / HEAD**0.5
    tok_two = jnp.concatenate([tok_col, tok_col], axis=0)
    tile = 2 * pre_rows
    seen = []
    tops = None
    wait_slot(pre_slot(0, 1 - y, c), p2s.at[0], p2r.at[0])
    send(pre_slot(0, 1 - y, c), pre_slot(0, 1 - y, c), pps.at[0, 1], ppr.at[0, 1], t, peer)
    remote(
        qall.at[pl.ds(0, tokens)], qall.at[pl.ds(tokens, tokens)], qs, qr, t, peer
    ).wait_recv()
    pieces = [(0, 0), (0, 1), (1, 0), (1, 1)]

    def piece_rows(which, rel):
        chip_row = y if rel == 0 else 1 - y
        return pl.ds(pl.multiple_of((which * 2 + chip_row) * tile, tile), tile)

    for i, (which, rel) in enumerate(pieces):
        chip_row = y if rel == 0 else 1 - y
        if (which, rel) == (1, 1):
            wait_slot(pre_slot(1, chip_row, c), p2s.at[1], p2r.at[1])
            slot = pre_slot(1, chip_row, c)
            send(slot, slot, pps.at[1, 1], ppr.at[1, 1], t, peer)
        wait_slot(pre_slot(which, chip_row, peer), pps.at[which, rel], ppr.at[which, rel])
        chip = (2 * (t // 2) + 4 * which) % chips + chip_row
        seg = segments(lax.broadcasted_iota(jnp.int32, (1, tile), 1) + chip * tile, plen_ref)
        seen.append(seg)
        raw = lax.dot_general(
            qall[...], kvbuf[piece_rows(which, rel), :HEAD], nt, preferred_element_type=F32
        )
        masked = jnp.where(tok_two == seg, raw * score_scale, negative)
        scores[:, i * tile : (i + 1) * tile] = masked
        top = jnp.max(masked, axis=1, keepdims=True)
        tops = top if tops is None else jnp.maximum(tops, top)

    def absorb(first_row):
        rows = slice(first_row, first_row + tokens)
        top = tops[rows]
        total = jnp.zeros((tokens, 1), F32)
        product = jnp.zeros((tokens, HEAD), F32)
        for i, (which, rel) in enumerate(pieces):
            weights = jnp.exp(scores[rows, i * tile : (i + 1) * tile] - top)
            weights = jnp.where(tok_col == seen[i], weights, 0.0)
            total = total + jnp.sum(weights, axis=1, keepdims=True)
            product = product + jnp.dot(
                weights.astype(BF16), kvbuf[piece_rows(which, rel), HEAD:], preferred_element_type=F32
            )
        return top, total, product

    top, total, product = absorb(tokens)
    lane = lax.broadcasted_iota(jnp.int32, (tokens, tokens), 1)
    turned = jnp.transpose(jnp.where(lane < tokens // 2, top, total))
    sums_out[:tokens, :] = product
    sums_out[tokens:, :] = turned[tokens // 2 - 8 : tokens // 2 + 8]
    send(sums_out, sums_in, ss, sr, along, c)
    top, total, product = absorb(0)

    for r in range(1, devices):
        slot = kv_slot((d + devices - r) % devices)
        remote(slot, slot, kvs.at[r], kvr.at[r], t, peer).wait_recv()
    key_base = pl.multiple_of(g * 2 * HEAD, 2 * HEAD)
    span_keys = kvt[pl.ds(key_base, HEAD), :]
    span_values = kvt[pl.ds(key_base + HEAD, HEAD), :]
    before = lax.broadcasted_iota(jnp.int32, (tokens, tokens), 0) >= lax.broadcasted_iota(
        jnp.int32, (tokens, tokens), 1
    )
    span_mask = (tok_col == tok_row) & before
    span_scores = jnp.where(
        span_mask, jnp.dot(queries, span_keys, preferred_element_type=F32) * score_scale, negative
    )
    remote(sums_out, sums_in, ss, sr, t, peer).wait_recv()
    turned = jnp.transpose(jnp.concatenate([sums_in[tokens:, :]] * (tokens // 16), axis=0))
    other_top, other_total = turned[:, 0:1], turned[:, 8:9]
    span_top = jnp.max(span_scores, axis=1, keepdims=True)
    row_max = jnp.maximum(jnp.maximum(top, other_top), span_top)
    weights = jnp.where(span_mask, jnp.exp(span_scores - row_max), 0.0)
    factor, other_factor = jnp.exp(top - row_max), jnp.exp(other_top - row_max)
    row_total = (
        jnp.sum(weights, axis=1, keepdims=True) + total * factor + other_total * other_factor
    )
    summed = lax.dot_general(weights.astype(BF16), span_values, nt, preferred_element_type=F32)
    summed = summed + product * factor + sums_in[:tokens, :] * other_factor
    attention = (summed / row_total).astype(BF16)

    loads[3].wait()
    step = 1024
    for i in range(width // step):
        part[:, i * step : (i + 1) * step] = jnp.dot(
            attention, wout[:, i * step : (i + 1) * step], preferred_element_type=F32
        )

    def stacked(k, core, h):
        rows = pl.ds(pl.multiple_of(16 * chip_at((pos + k) % chips, chips) + 8 * core, 8), 8)
        top = part[rows, h * quarter : (h + 1) * quarter]
        bottom = part[rows, half + h * quarter : half + (h + 1) * quarter]
        return jnp.concatenate([top, bottom], axis=0)

    order = [4, 3, 5, 2, 6, 1, 7, 0]
    for k in order:
        for h in range(2):
            peer_out[k, :, h * quarter : (h + 1) * quarter] = stacked(k, peer, h).astype(BF16)
        send(peer_out.at[k], peer_in.at[k], pes.at[k], per.at[k], t, peer)

    def summand(k, h):
        return stacked(k, c, h) + peer_in[k, :, h * quarter : (h + 1) * quarter].astype(F32)

    def from_peer(k):
        remote(peer_out.at[k], peer_in.at[k], pes.at[k], per.at[k], t, peer).wait_recv()

    def from_ring(way, s, h):
        remote(
            ring_out.at[way, s, h], ring_in.at[way, s, h], rss.at[way, s, h], rsr.at[way, s, h], nxt, c
        ).wait_recv()
        return ring_in[way, s, h].astype(F32)

    hops = [(s, h, way) for s in range(4) for h in range(2) for way in (CW, CCW)]
    hops = [m for m in hops if m[0] > 0 or m[1] == m[2]]
    hops = [m for m in hops if m[0] == 0] + sorted(
        [m for m in hops if m[0] > 0], key=lambda m: (m[0], m[1] == m[2])
    )
    ready = []
    for s, h, way in hops:
        k = 4 - s if way == CW else 4 + s
        if k not in ready:
            from_peer(k)
            ready.append(k)
        value = summand(k, h)
        if (s - 1, h, way) in hops:
            value = value + from_ring(way, s - 1, h)
        ring_out[way, s, h] = value.astype(BF16)
        send(
            ring_out.at[way, s, h],
            ring_in.at[way, s, h],
            rss.at[way, s, h],
            rsr.at[way, s, h],
            (nxt, prv)[way],
            c,
        )

    first_row = 0
    length = 0
    target = 0
    start = 0
    for r in range(span_ref.shape[0]):
        own_it = (owner_ref[r] == d).astype(jnp.int32)
        first_row = first_row + own_it * start
        length = length + own_it * span_ref[r]
        target = target + own_it * offset_ref[r]
        start = start + span_ref[r]
    loads[4].wait()
    cache_rows = dec.shape[0]
    row = lax.broadcasted_iota(jnp.int32, (cache_rows, tokens), 0) - target
    token = lax.broadcasted_iota(jnp.int32, (cache_rows, tokens), 1)
    picks = ((token - first_row) == row) & (row >= 0) & (row < length)
    picked = lax.dot_general(
        picks.astype(F32).astype(BF16), kvt[...], nt, preferred_element_type=F32
    )
    row = lax.broadcasted_iota(jnp.int32, (cache_rows, 1), 0) - target
    written = jnp.where((row >= 0) & (row < length), picked, dec[...].astype(F32))
    cache_ref[...] = written.astype(BF16)

    from_peer(0)
    for h in range(2):
        value = summand(0, h) + from_ring(CW, 3, h) + from_ring(CCW, 3, h)
        for side in range(2):
            columns = slice(side * half + h * quarter, side * half + (h + 1) * quarter)
            out_ref[:, columns] = (
                x_ref[:, columns].astype(F32) + value[8 * side : 8 * side + 8]
            ).astype(BF16)
    for copy in sent:
        copy.wait_send()


def fused_shards(
    stream_in,
    norm_gain,
    w_query,
    w_keyval,
    w_out,
    prefix_cache,
    span_lens,
    prefix_lens,
    owner_dev,
    offsets,
    decode_cache,
):
    chips = lax.axis_size("tensor")
    devices = 2 * chips
    rows, width = stream_in.shape
    tokens = rows * devices
    pre_rows = prefix_cache.shape[0]
    quarter = width // 4
    vmem = pl.BlockSpec(memory_space=pltpu.VMEM)
    smem = pl.BlockSpec(memory_space=pltpu.SMEM)
    hbm = pl.BlockSpec(memory_space=pl.ANY)
    dma = pltpu.SemaphoreType.DMA
    return pl.pallas_call(
        fused,
        out_shape=(
            jax.ShapeDtypeStruct(stream_in.shape, BF16),
            jax.ShapeDtypeStruct(decode_cache.shape, BF16),
        ),
        in_specs=[vmem, vmem] + [smem] * 4 + [hbm] * 5,
        out_specs=(vmem, vmem),
        scratch_shapes=[
            pltpu.VMEM(w_query.shape, BF16),
            pltpu.VMEM((w_keyval.shape[1], width), BF16),
            pltpu.VMEM(w_out.shape, BF16),
            pltpu.VMEM(decode_cache.shape, BF16),
            pltpu.VMEM((tokens, width), BF16),
            pltpu.VMEM((8, width // 2), BF16),
            pltpu.VMEM((8, width // 2), BF16),
            pltpu.VMEM((devices // 2 * pre_rows, 2 * HEAD), BF16),
            pltpu.VMEM((devices * w_keyval.shape[1], tokens), BF16),
            pltpu.VMEM((2 * tokens, HEAD), BF16),
            pltpu.VMEM((tokens + 16, HEAD), F32),
            pltpu.VMEM((tokens + 16, HEAD), F32),
            pltpu.VMEM((2 * tokens, devices // 2 * pre_rows), F32),
            pltpu.VMEM((tokens, width), F32),
            pltpu.VMEM((chips, 16, width // 2), BF16),
            pltpu.VMEM((chips, 16, width // 2), BF16),
            pltpu.VMEM((2, 4, 2, 16, quarter), BF16),
            pltpu.VMEM((2, 4, 2, 16, quarter), BF16),
            dma((5,)),
            dma,
            dma,
            dma((2, 4, 2)),
            dma((2, 4, 2)),
            dma((2, 4, 2)),
            dma((2, 4, 2)),
            dma,
            dma,
            dma((2,)),
            dma((2,)),
            dma((2, 2)),
            dma((2, 2)),
            dma((devices,)),
            dma((devices,)),
            dma,
            dma,
            dma,
            dma,
            dma((chips,)),
            dma((chips,)),
            dma((2, 4, 2)),
            dma((2, 4, 2)),
        ],
        compiler_params=pltpu.CompilerParams(
            collective_id=0, has_side_effects=True, vmem_limit_bytes=60 * 1024 * 1024
        ),
        name="fused_attention",
    )(
        stream_in,
        norm_gain,
        span_lens,
        prefix_lens,
        owner_dev,
        offsets,
        w_query,
        w_keyval.T,
        w_out,
        prefix_cache,
        decode_cache,
    )


def solution(mesh):
    in_specs = (
        P(("groups", "tensor", "role"), None),
        P(),
        P(None, ("tensor", "role")),
        P(None, ("tensor", "role")),
        P(("tensor", "role"), None),
        P(("groups", "tensor", "role"), None),
        P("groups"),
        P("groups"),
        P("groups"),
        P("groups"),
        P(("groups", "tensor", "role"), None),
    )
    out_specs = (P(("groups", "tensor", "role"), None), P(("groups", "tensor", "role"), None))
    small = mesh.shape["tensor"] == 8 and mesh.shape["role"] == 2
    body = fused_shards if small else shards
    return jax.shard_map(body, mesh=mesh, in_specs=in_specs, out_specs=out_specs, check_vma=False)
```

```python
import jax
import jax.numpy as jnp
from jax import lax
from jax.experimental import pallas as pl
from jax.experimental.pallas import tpu as pltpu
from jax.sharding import PartitionSpec as P

HEAD = 128
GROUP = 8


epsilon = 1e-05
negative = -1e30


def segment_of(positions, lengths):
    run_ends = jnp.cumsum(lengths)
    return jnp.sum((positions[:, None] >= run_ends[None, :]).astype(jnp.int32), axis=1)


def shards(
    stream_in,
    norm_gain,
    w_query,
    w_keyval,
    w_out,
    prefix_cache,
    span_lens,
    prefix_lens,
    owner_dev,
    offsets,
    decode_cache,
):
    devices = lax.axis_size(("tensor", "role"))
    myself = lax.axis_index(("tensor", "role"))
    span_rows = stream_in.shape[0] * devices
    local_pre = prefix_cache.shape[0]
    kv_heads = devices // GROUP
    score_scale = 1.0 / HEAD**0.5
    floats = stream_in.astype(jnp.float32)
    normed = (
        floats
        * lax.rsqrt(jnp.mean(floats * floats, axis=1, keepdims=True) + epsilon)
        * norm_gain.astype(jnp.float32)
    ).astype(jnp.bfloat16)
    shard_rows = lax.all_gather(normed, ("tensor", "role"), axis=0, tiled=True)
    projected = jnp.concatenate(
        [
            jnp.dot(shard_rows, w_query, preferred_element_type=jnp.float32),
            jnp.dot(shard_rows, w_keyval, preferred_element_type=jnp.float32),
        ],
        axis=1,
    )
    queries = projected[:, :HEAD].astype(jnp.bfloat16)
    kv_local = projected[:, HEAD:].astype(jnp.bfloat16)
    keyval = lax.all_gather(kv_local, ("tensor", "role"), axis=1, tiled=True)
    column_base = myself // GROUP * (2 * HEAD)
    span_keys = lax.dynamic_slice_in_dim(keyval, column_base, HEAD, 1)
    span_values = lax.dynamic_slice_in_dim(keyval, column_base + HEAD, HEAD, 1)
    row_index = jnp.arange(span_rows, dtype=jnp.int32)
    tok_seg = segment_of(row_index, span_lens)
    span_mask = (tok_seg[:, None] == tok_seg[None, :]) & (row_index[:, None] >= row_index[None, :])
    span_scores = jnp.where(
        span_mask,
        jnp.dot(queries, span_keys.T, preferred_element_type=jnp.float32) * score_scale,
        negative,
    )
    stored = jnp.transpose(prefix_cache.reshape(local_pre, kv_heads, 2 * HEAD), (1, 0, 2))
    span_max = jnp.max(span_scores, axis=1)
    span_weights = jnp.where(span_mask, jnp.exp(span_scores - span_max[:, None]), 0.0)
    start_carry = (
        span_max,
        jnp.sum(span_weights, axis=1),
        jnp.dot(span_weights.astype(jnp.bfloat16), span_values, preferred_element_type=jnp.float32),
    )
    repeated = jnp.repeat(stored, GROUP, axis=0)
    received = lax.all_to_all(repeated, ("tensor", "role"), split_axis=0, concat_axis=1, tiled=True)
    all_rows = devices * local_pre
    factor_count = 1
    while devices % (factor_count * 2) == 0 and factor_count * 2 * local_pre <= 512:
        factor_count = factor_count * 2
    block_rows = factor_count * local_pre
    blocks = received.reshape(all_rows // block_rows, block_rows, 2 * HEAD)

    def absorb(running, block_pair):
        row_max, row_total, summed = running
        block_number, shard_rows = block_pair
        row_start = block_number * block_rows
        key_seg = segment_of(row_start + jnp.arange(block_rows, dtype=jnp.int32), prefix_lens)
        visible = tok_seg[:, None] == key_seg[None, :]
        key_rows = shard_rows[:, :HEAD]
        value_rows = shard_rows[:, HEAD:]
        scores = jnp.where(
            visible,
            jnp.dot(queries, key_rows.T, preferred_element_type=jnp.float32) * score_scale,
            negative,
        )
        new_max = jnp.maximum(row_max, jnp.max(scores, axis=1))
        factor = jnp.exp(row_max - new_max)
        weights = jnp.where(visible, jnp.exp(scores - new_max[:, None]), 0.0)
        summed = summed * factor[:, None] + jnp.dot(
            weights.astype(jnp.bfloat16), value_rows, preferred_element_type=jnp.float32
        )
        return ((new_max, row_total * factor + jnp.sum(weights, axis=1), summed), None)

    numbers = jnp.arange(all_rows // block_rows, dtype=jnp.int32)
    (row_max, row_total, summed), unused = lax.scan(absorb, start_carry, (numbers, blocks))
    attention = (summed / row_total[:, None]).astype(jnp.bfloat16)
    stream_out = (
        floats
        + lax.psum_scatter(
            jnp.dot(attention, w_out, preferred_element_type=jnp.float32),
            ("tensor", "role"),
            scatter_dimension=0,
            tiled=True,
        )
    ).astype(jnp.bfloat16)
    owned = owner_dev == myself
    owned_count = jnp.sum(owned.astype(jnp.int32))
    starts = jnp.cumsum(span_lens) - span_lens
    first_row = jnp.sum(jnp.where(owned, starts, 0))
    length = jnp.sum(jnp.where(owned, span_lens, 0))
    target = jnp.sum(jnp.where(owned, offsets, 0))
    padded = jnp.concatenate(
        [keyval, jnp.zeros((span_rows, keyval.shape[1]), jnp.bfloat16)], axis=0
    )
    kv_block = lax.dynamic_slice_in_dim(padded, first_row, span_rows, 0)
    before = lax.dynamic_slice_in_dim(decode_cache, target, span_rows, 0)
    keep_new = (row_index < length) & (owned_count > 0)
    written = jnp.where(keep_new[:, None], kv_block, before)
    cache_out = lax.dynamic_update_slice_in_dim(decode_cache, written, target, 0)
    return (stream_out, cache_out)


MESH = pl.DeviceIdType.MESH
F32 = jnp.float32
BF16 = jnp.bfloat16
CW, CCW = 0, 1


def chip_at(position, chips):
    back = position // (chips // 2)
    return (1 - back) * 2 * position + back * (2 * (chips - 1 - position) + 1)


def fused(
    x_ref,
    gain_ref,
    span_ref,
    plen_ref,
    owner_ref,
    offset_ref,
    wq_hbm,
    wkv_hbm,
    wout_hbm,
    pre_hbm,
    dec_hbm,
    out_ref,
    cache_ref,
    wq,
    wkv,
    wout,
    dec,
    normed,
    xsend,
    xrecv,
    kvbuf,
    kvt,
    qall,
    sums_out,
    sums_in,
    scores,
    part,
    peer_out,
    peer_in,
    ring_out,
    ring_in,
    lsem,
    xs,
    xr,
    ags,
    agr,
    pfs,
    pfr,
    p1s,
    p1r,
    p2s,
    p2r,
    pps,
    ppr,
    kvs,
    kvr,
    qs,
    qr,
    ss,
    sr,
    pes,
    per,
    rss,
    rsr,
):
    chips = lax.axis_size("tensor")
    devices = 2 * chips
    t = lax.axis_index("tensor")
    c = lax.axis_index("role")
    peer = 1 - c
    d = 2 * t + c
    odd = t % 2
    pos = (1 - odd) * (t // 2) + odd * (chips - 1 - t // 2)
    nxt = chip_at((pos + 1) % chips, chips)
    prv = chip_at((pos + chips - 1) % chips, chips)
    width = x_ref.shape[1]
    half = width // 2
    quarter = width // 4
    tokens = 16 * chips
    pre_rows = pre_hbm.shape[0]
    g = t // 4
    y = t % 2
    across = t + 1 - 2 * y
    along = t + 2 - 4 * ((t // 2) % 2)

    def remote(src, dst, ssem, rsem, tt, cc):
        return pltpu.make_async_remote_copy(
            src_ref=src,
            dst_ref=dst,
            send_sem=ssem,
            recv_sem=rsem,
            device_id={"tensor": tt, "role": cc},
            device_id_type=MESH,
        )

    sent = []

    def send(*args):
        copy = remote(*args)
        copy.start()
        sent.append(copy)

    barrier = pltpu.get_barrier_semaphore()
    for r in range(1, devices):
        other = (d + r) % devices
        pl.semaphore_signal(
            barrier, inc=1, device_id={"tensor": other // 2, "role": other % 2}, device_id_type=MESH
        )

    def pre_slot(which, row, core):
        index = which * 4 + row * 2 + core
        return kvbuf.at[pl.ds(pl.multiple_of(index * pre_rows, pre_rows), pre_rows), :]

    def head_columns(head):
        return pre_hbm.at[:, pl.ds(pl.multiple_of(head * 2 * HEAD, 2 * HEAD), 2 * HEAD)]

    loads = [
        pltpu.make_async_copy(head_columns(g), pre_slot(0, y, c), lsem.at[0]),
        pltpu.make_async_copy(wkv_hbm, wkv, lsem.at[1]),
        pltpu.make_async_copy(wq_hbm, wq, lsem.at[2]),
        pltpu.make_async_copy(wout_hbm, wout, lsem.at[3]),
        pltpu.make_async_copy(dec_hbm, dec, lsem.at[4]),
    ]
    for load in loads:
        load.start()

    floats = x_ref[...].astype(F32)
    mine = floats * lax.rsqrt(jnp.mean(floats * floats, axis=1, keepdims=True) + epsilon)
    mine = mine * gain_ref[...].astype(F32).reshape(1, width)
    is_one = (c == 1).astype(F32)
    left, right = mine[:, :half], mine[:, half:]
    xsend[...] = jnp.where(is_one > 0.5, left, right).astype(BF16)
    kept = jnp.where(is_one > 0.5, right, left).astype(BF16).astype(F32)

    pl.semaphore_wait(barrier, devices - 1)
    send(xsend, xrecv, xs, xr, t, peer)

    def block(chip, core, h=None):
        column = core * half if h is None else core * half + h * quarter
        size = half if h is None else quarter
        return (
            pl.ds(pl.multiple_of(16 * chip, 16), 16),
            pl.ds(pl.multiple_of(column, quarter), size),
        )

    remote(xsend, xrecv, xs, xr, t, peer).wait_recv()
    theirs = xrecv[...].astype(F32)
    first = jnp.where(is_one > 0.5, theirs, kept)
    second = jnp.where(is_one > 0.5, kept, theirs)
    normed[block(t, c)] = jnp.concatenate([first, second], axis=0).astype(BF16)

    def source(way, hops):
        return chip_at((pos + chips - hops) % chips if way == CW else (pos + hops) % chips, chips)

    def hop(way, s, h):
        here = normed.at[block(source(way, s), c, h)]
        send(here, here, ags.at[way, s, h], agr.at[way, s, h], (nxt, prv)[way], c)

    last = chips // 2 - 1
    own = normed.at[block(t, c)]
    messages = [(s, h, way) for s in range(last + 1) for h in range(2) for way in (CW, CCW)]
    messages = [m for m in messages if m[0] < last or m[1] == m[2]]
    messages = sorted(messages, key=lambda m: (m[0], m[1] != m[2]))
    for s, h, way in messages:
        if s == 0:
            hop(way, 0, h)
    send(own, own, pfs.at[0, last, 1], pfr.at[0, last, 1], t, peer)
    for s, h, way in messages:
        landed = normed.at[block(source(way, s + 1), c, h)]
        remote(landed, landed, ags.at[way, s, h], agr.at[way, s, h], nxt, c).wait_recv()
        if (s + 1, h, way) in messages:
            hop(way, s + 1, h)
        send(landed, landed, pfs.at[way, s, h], pfr.at[way, s, h], t, peer)
        if (s, h, way) == (last - 1, 0, CCW):
            send(head_columns(1 - g), pre_slot(1, y, c), p1s, p1r, (t + 4) % chips, c)

    loads[0].wait()

    def spread(which):
        slot = pre_slot(which, y, c)
        send(slot, slot, p2s.at[which], p2r.at[which], across, c)
        send(slot, slot, pps.at[which, 0], ppr.at[which, 0], t, peer)

    spread(0)

    own = normed.at[block(t, peer)]
    remote(own, own, pfs.at[0, last, 1], pfr.at[0, last, 1], t, peer).wait_recv()
    for s, h, way in messages:
        landed = normed.at[block(source(way, s + 1), peer, h)]
        remote(landed, landed, pfs.at[way, s, h], pfr.at[way, s, h], t, peer).wait_recv()
    loads[1].wait()
    nt = (((1,), (1,)), ((), ()))
    kv = lax.dot_general(wkv[...], normed[...], nt, preferred_element_type=F32)
    kv_rows = wkv.shape[0]

    def kv_slot(index):
        return kvt.at[pl.ds(pl.multiple_of(index * kv_rows, kv_rows), kv_rows), :]

    kv_slot(d)[...] = kv.astype(BF16)
    for r in range(1, devices):
        other = (d + r) % devices
        send(kv_slot(d), kv_slot(d), kvs.at[r], kvr.at[r], other // 2, other % 2)
    loads[2].wait()
    queries = jnp.dot(normed[...], wq[...], preferred_element_type=F32).astype(BF16)
    qall[:tokens, :] = queries
    send(qall.at[pl.ds(0, tokens)], qall.at[pl.ds(tokens, tokens)], qs, qr, along, c)
    slot = pre_slot(1, y, c)
    remote(slot, slot, p1s, p1r, t, peer).wait_recv()
    spread(1)

    def segments(positions, ref):
        end = 0
        total = jnp.zeros_like(positions)
        for r in range(ref.shape[0]):
            end = end + ref[r]
            total = total + (positions >= end).astype(jnp.int32)
        return total

    tok_col = segments(lax.broadcasted_iota(jnp.int32, (tokens, 1), 0), span_ref)
    tok_row = segments(lax.broadcasted_iota(jnp.int32, (1, tokens), 1), span_ref)

    def wait_slot(slot, ssem, rsem):
        remote(slot, slot, ssem, rsem, t, peer).wait_recv()

    score_scale = 1.0 / HEAD**0.5
    tok_two = jnp.concatenate([tok_col, tok_col], axis=0)
    tile = 2 * pre_rows
    seen = []
    tops = None
    wait_slot(pre_slot(0, 1 - y, c), p2s.at[0], p2r.at[0])
    send(pre_slot(0, 1 - y, c), pre_slot(0, 1 - y, c), pps.at[0, 1], ppr.at[0, 1], t, peer)
    remote(
        qall.at[pl.ds(0, tokens)], qall.at[pl.ds(tokens, tokens)], qs, qr, t, peer
    ).wait_recv()
    pieces = [(0, 0), (0, 1), (1, 0), (1, 1)]

    def piece_rows(which, rel):
        chip_row = y if rel == 0 else 1 - y
        return pl.ds(pl.multiple_of((which * 2 + chip_row) * tile, tile), tile)

    for i, (which, rel) in enumerate(pieces):
        chip_row = y if rel == 0 else 1 - y
        if (which, rel) == (1, 1):
            wait_slot(pre_slot(1, chip_row, c), p2s.at[1], p2r.at[1])
            slot = pre_slot(1, chip_row, c)
            send(slot, slot, pps.at[1, 1], ppr.at[1, 1], t, peer)
        wait_slot(pre_slot(which, chip_row, peer), pps.at[which, rel], ppr.at[which, rel])
        chip = (2 * (t // 2) + 4 * which) % chips + chip_row
        seg = segments(lax.broadcasted_iota(jnp.int32, (1, tile), 1) + chip * tile, plen_ref)
        seen.append(seg)
        raw = lax.dot_general(
            qall[...], kvbuf[piece_rows(which, rel), :HEAD], nt, preferred_element_type=F32
        )
        masked = jnp.where(tok_two == seg, raw * score_scale, negative)
        scores[:, i * tile : (i + 1) * tile] = masked
        top = jnp.max(masked, axis=1, keepdims=True)
        tops = top if tops is None else jnp.maximum(tops, top)

    def absorb(first_row):
        rows = slice(first_row, first_row + tokens)
        top = tops[rows]
        total = jnp.zeros((tokens, 1), F32)
        product = jnp.zeros((tokens, HEAD), F32)
        for i, (which, rel) in enumerate(pieces):
            weights = jnp.exp(scores[rows, i * tile : (i + 1) * tile] - top)
            weights = jnp.where(tok_col == seen[i], weights, 0.0)
            total = total + jnp.sum(weights, axis=1, keepdims=True)
            product = product + jnp.dot(
                weights.astype(BF16), kvbuf[piece_rows(which, rel), HEAD:], preferred_element_type=F32
            )
        return top, total, product

    top, total, product = absorb(tokens)
    lane = lax.broadcasted_iota(jnp.int32, (tokens, tokens), 1)
    turned = jnp.transpose(jnp.where(lane < tokens // 2, top, total))
    sums_out[:tokens, :] = product
    sums_out[tokens:, :] = turned[tokens // 2 - 8 : tokens // 2 + 8]
    send(sums_out, sums_in, ss, sr, along, c)
    top, total, product = absorb(0)

    for r in range(1, devices):
        slot = kv_slot((d + devices - r) % devices)
        remote(slot, slot, kvs.at[r], kvr.at[r], t, peer).wait_recv()
    key_base = pl.multiple_of(g * 2 * HEAD, 2 * HEAD)
    span_keys = kvt[pl.ds(key_base, HEAD), :]
    span_values = kvt[pl.ds(key_base + HEAD, HEAD), :]
    before = lax.broadcasted_iota(jnp.int32, (tokens, tokens), 0) >= lax.broadcasted_iota(
        jnp.int32, (tokens, tokens), 1
    )
    span_mask = (tok_col == tok_row) & before
    span_scores = jnp.where(
        span_mask, jnp.dot(queries, span_keys, preferred_element_type=F32) * score_scale, negative
    )
    remote(sums_out, sums_in, ss, sr, t, peer).wait_recv()
    turned = jnp.transpose(jnp.concatenate([sums_in[tokens:, :]] * (tokens // 16), axis=0))
    other_top, other_total = turned[:, 0:1], turned[:, 8:9]
    span_top = jnp.max(span_scores, axis=1, keepdims=True)
    row_max = jnp.maximum(jnp.maximum(top, other_top), span_top)
    weights = jnp.where(span_mask, jnp.exp(span_scores - row_max), 0.0)
    factor, other_factor = jnp.exp(top - row_max), jnp.exp(other_top - row_max)
    row_total = (
        jnp.sum(weights, axis=1, keepdims=True) + total * factor + other_total * other_factor
    )
    summed = lax.dot_general(weights.astype(BF16), span_values, nt, preferred_element_type=F32)
    summed = summed + product * factor + sums_in[:tokens, :] * other_factor
    attention = (summed / row_total).astype(BF16)

    loads[3].wait()
    step = 1024
    for i in range(width // step):
        part[:, i * step : (i + 1) * step] = jnp.dot(
            attention, wout[:, i * step : (i + 1) * step], preferred_element_type=F32
        )

    def stacked(k, core, h):
        rows = pl.ds(pl.multiple_of(16 * chip_at((pos + k) % chips, chips) + 8 * core, 8), 8)
        top = part[rows, h * quarter : (h + 1) * quarter]
        bottom = part[rows, half + h * quarter : half + (h + 1) * quarter]
        return jnp.concatenate([top, bottom], axis=0)

    order = [4, 3, 5, 2, 6, 1, 7, 0]
    for k in order:
        for h in range(2):
            peer_out[k, :, h * quarter : (h + 1) * quarter] = stacked(k, peer, h).astype(BF16)
        send(peer_out.at[k], peer_in.at[k], pes.at[k], per.at[k], t, peer)

    def summand(k, h):
        return stacked(k, c, h) + peer_in[k, :, h * quarter : (h + 1) * quarter].astype(F32)

    def from_peer(k):
        remote(peer_out.at[k], peer_in.at[k], pes.at[k], per.at[k], t, peer).wait_recv()

    def from_ring(way, s, h):
        remote(
            ring_out.at[way, s, h], ring_in.at[way, s, h], rss.at[way, s, h], rsr.at[way, s, h], nxt, c
        ).wait_recv()
        return ring_in[way, s, h].astype(F32)

    hops = [(s, h, way) for s in range(4) for h in range(2) for way in (CW, CCW)]
    hops = [m for m in hops if m[0] > 0 or m[1] == m[2]]
    hops = [m for m in hops if m[0] == 0] + sorted(
        [m for m in hops if m[0] > 0], key=lambda m: (m[0], m[1] == m[2])
    )
    ready = []
    for s, h, way in hops:
        k = 4 - s if way == CW else 4 + s
        if k not in ready:
            from_peer(k)
            ready.append(k)
        value = summand(k, h)
        if (s - 1, h, way) in hops:
            value = value + from_ring(way, s - 1, h)
        ring_out[way, s, h] = value.astype(BF16)
        send(
            ring_out.at[way, s, h],
            ring_in.at[way, s, h],
            rss.at[way, s, h],
            rsr.at[way, s, h],
            (nxt, prv)[way],
            c,
        )

    first_row = 0
    length = 0
    target = 0
    start = 0
    for r in range(span_ref.shape[0]):
        own_it = (owner_ref[r] == d).astype(jnp.int32)
        first_row = first_row + own_it * start
        length = length + own_it * span_ref[r]
        target = target + own_it * offset_ref[r]
        start = start + span_ref[r]
    loads[4].wait()
    cache_rows = dec.shape[0]
    row = lax.broadcasted_iota(jnp.int32, (cache_rows, tokens), 0) - target
    token = lax.broadcasted_iota(jnp.int32, (cache_rows, tokens), 1)
    picks = ((token - first_row) == row) & (row >= 0) & (row < length)
    picked = lax.dot_general(
        picks.astype(F32).astype(BF16), kvt[...], nt, preferred_element_type=F32
    )
    row = lax.broadcasted_iota(jnp.int32, (cache_rows, 1), 0) - target
    written = jnp.where((row >= 0) & (row < length), picked, dec[...].astype(F32))
    cache_ref[...] = written.astype(BF16)

    from_peer(0)
    for h in range(2):
        value = summand(0, h) + from_ring(CW, 3, h) + from_ring(CCW, 3, h)
        for side in range(2):
            columns = slice(side * half + h * quarter, side * half + (h + 1) * quarter)
            out_ref[:, columns] = (
                x_ref[:, columns].astype(F32) + value[8 * side : 8 * side + 8]
            ).astype(BF16)
    for copy in sent:
        copy.wait_send()


def hand_over(stream_ref, cache_ref, stream_out, cache_out, stream_held, cache_held, sems):
    pairs = [
        (stream_ref, stream_held, stream_out),
        (cache_ref, cache_held, cache_out),
    ]
    into = [pltpu.make_async_copy(a, b, sems.at[i]) for i, (a, b, _) in enumerate(pairs)]
    out = [pltpu.make_async_copy(b, e, sems.at[2 + i]) for i, (_, b, e) in enumerate(pairs)]
    for copy in into:
        copy.start()
    for arrival, departure in zip(into, out):
        arrival.wait()
        departure.start()
    for copy in out:
        copy.wait()


def fused_shards(
    stream_in,
    norm_gain,
    w_query,
    w_keyval,
    w_out,
    prefix_cache,
    span_lens,
    prefix_lens,
    owner_dev,
    offsets,
    decode_cache,
):
    chips = lax.axis_size("tensor")
    devices = 2 * chips
    rows, width = stream_in.shape
    tokens = rows * devices
    pre_rows = prefix_cache.shape[0]
    quarter = width // 4
    vmem = pl.BlockSpec(memory_space=pltpu.VMEM)
    smem = pl.BlockSpec(memory_space=pltpu.SMEM)
    hbm = pl.BlockSpec(memory_space=pl.ANY)
    dma = pltpu.SemaphoreType.DMA
    results = pl.pallas_call(
        fused,
        out_shape=(
            jax.ShapeDtypeStruct(stream_in.shape, BF16),
            jax.ShapeDtypeStruct(decode_cache.shape, BF16),
        ),
        in_specs=[vmem, vmem] + [smem] * 4 + [hbm] * 5,
        out_specs=(vmem, vmem),
        scratch_shapes=[
            pltpu.VMEM(w_query.shape, BF16),
            pltpu.VMEM((w_keyval.shape[1], width), BF16),
            pltpu.VMEM(w_out.shape, BF16),
            pltpu.VMEM(decode_cache.shape, BF16),
            pltpu.VMEM((tokens, width), BF16),
            pltpu.VMEM((8, width // 2), BF16),
            pltpu.VMEM((8, width // 2), BF16),
            pltpu.VMEM((devices // 2 * pre_rows, 2 * HEAD), BF16),
            pltpu.VMEM((devices * w_keyval.shape[1], tokens), BF16),
            pltpu.VMEM((2 * tokens, HEAD), BF16),
            pltpu.VMEM((tokens + 16, HEAD), F32),
            pltpu.VMEM((tokens + 16, HEAD), F32),
            pltpu.VMEM((2 * tokens, devices // 2 * pre_rows), F32),
            pltpu.VMEM((tokens, width), F32),
            pltpu.VMEM((chips, 16, width // 2), BF16),
            pltpu.VMEM((chips, 16, width // 2), BF16),
            pltpu.VMEM((2, 4, 2, 16, quarter), BF16),
            pltpu.VMEM((2, 4, 2, 16, quarter), BF16),
            dma((5,)),
            dma,
            dma,
            dma((2, 4, 2)),
            dma((2, 4, 2)),
            dma((2, 4, 2)),
            dma((2, 4, 2)),
            dma,
            dma,
            dma((2,)),
            dma((2,)),
            dma((2, 2)),
            dma((2, 2)),
            dma((devices,)),
            dma((devices,)),
            dma,
            dma,
            dma,
            dma,
            dma((chips,)),
            dma((chips,)),
            dma((2, 4, 2)),
            dma((2, 4, 2)),
        ],
        compiler_params=pltpu.CompilerParams(
            collective_id=0, has_side_effects=True, vmem_limit_bytes=60 * 1024 * 1024
        ),
        name="fused_attention",
    )(
        stream_in,
        norm_gain,
        span_lens,
        prefix_lens,
        owner_dev,
        offsets,
        w_query,
        w_keyval.T,
        w_out,
        prefix_cache,
        decode_cache,
    )
    return pl.pallas_call(
        hand_over,
        out_shape=(
            jax.ShapeDtypeStruct(stream_in.shape, BF16),
            jax.ShapeDtypeStruct(decode_cache.shape, BF16),
        ),
        in_specs=[hbm, hbm],
        out_specs=(hbm, hbm),
        scratch_shapes=[
            pltpu.VMEM(stream_in.shape, BF16),
            pltpu.VMEM(decode_cache.shape, BF16),
            dma((4,)),
        ],
        name="hand_over",
    )(*results)


def solution(mesh):
    in_specs = (
        P(("groups", "tensor", "role"), None),
        P(),
        P(None, ("tensor", "role")),
        P(None, ("tensor", "role")),
        P(("tensor", "role"), None),
        P(("groups", "tensor", "role"), None),
        P("groups"),
        P("groups"),
        P("groups"),
        P("groups"),
        P(("groups", "tensor", "role"), None),
    )
    out_specs = (P(("groups", "tensor", "role"), None), P(("groups", "tensor", "role"), None))
    small = mesh.shape["tensor"] == 8 and mesh.shape["role"] == 2
    body = fused_shards if small else shards
    return jax.shard_map(body, mesh=mesh, in_specs=in_specs, out_specs=out_specs, check_vma=False)
```

```python
import jax
import jax.numpy as jnp
from jax import lax
from jax.experimental import pallas as pl
from jax.experimental.pallas import tpu as pltpu
from jax.sharding import PartitionSpec as P

HEAD = 128
GROUP = 8


epsilon = 1e-05
negative = -1e30


def segment_of(positions, lengths):
    run_ends = jnp.cumsum(lengths)
    return jnp.sum((positions[:, None] >= run_ends[None, :]).astype(jnp.int32), axis=1)


def shards(
    stream_in,
    norm_gain,
    w_query,
    w_keyval,
    w_out,
    prefix_cache,
    span_lens,
    prefix_lens,
    owner_dev,
    offsets,
    decode_cache,
):
    devices = lax.axis_size(("tensor", "role"))
    myself = lax.axis_index(("tensor", "role"))
    span_rows = stream_in.shape[0] * devices
    local_pre = prefix_cache.shape[0]
    kv_heads = devices // GROUP
    score_scale = 1.0 / HEAD**0.5
    floats = stream_in.astype(jnp.float32)
    normed = (
        floats
        * lax.rsqrt(jnp.mean(floats * floats, axis=1, keepdims=True) + epsilon)
        * norm_gain.astype(jnp.float32)
    ).astype(jnp.bfloat16)
    shard_rows = lax.all_gather(normed, ("tensor", "role"), axis=0, tiled=True)
    projected = jnp.concatenate(
        [
            jnp.dot(shard_rows, w_query, preferred_element_type=jnp.float32),
            jnp.dot(shard_rows, w_keyval, preferred_element_type=jnp.float32),
        ],
        axis=1,
    )
    queries = projected[:, :HEAD].astype(jnp.bfloat16)
    kv_local = projected[:, HEAD:].astype(jnp.bfloat16)
    keyval = lax.all_gather(kv_local, ("tensor", "role"), axis=1, tiled=True)
    column_base = myself // GROUP * (2 * HEAD)
    span_keys = lax.dynamic_slice_in_dim(keyval, column_base, HEAD, 1)
    span_values = lax.dynamic_slice_in_dim(keyval, column_base + HEAD, HEAD, 1)
    row_index = jnp.arange(span_rows, dtype=jnp.int32)
    tok_seg = segment_of(row_index, span_lens)
    span_mask = (tok_seg[:, None] == tok_seg[None, :]) & (row_index[:, None] >= row_index[None, :])
    span_scores = jnp.where(
        span_mask,
        jnp.dot(queries, span_keys.T, preferred_element_type=jnp.float32) * score_scale,
        negative,
    )
    stored = jnp.transpose(prefix_cache.reshape(local_pre, kv_heads, 2 * HEAD), (1, 0, 2))
    span_max = jnp.max(span_scores, axis=1)
    span_weights = jnp.where(span_mask, jnp.exp(span_scores - span_max[:, None]), 0.0)
    start_carry = (
        span_max,
        jnp.sum(span_weights, axis=1),
        jnp.dot(span_weights.astype(jnp.bfloat16), span_values, preferred_element_type=jnp.float32),
    )
    repeated = jnp.repeat(stored, GROUP, axis=0)
    received = lax.all_to_all(repeated, ("tensor", "role"), split_axis=0, concat_axis=1, tiled=True)
    all_rows = devices * local_pre
    factor_count = 1
    while devices % (factor_count * 2) == 0 and factor_count * 2 * local_pre <= 512:
        factor_count = factor_count * 2
    block_rows = factor_count * local_pre
    blocks = received.reshape(all_rows // block_rows, block_rows, 2 * HEAD)

    def absorb(running, block_pair):
        row_max, row_total, summed = running
        block_number, shard_rows = block_pair
        row_start = block_number * block_rows
        key_seg = segment_of(row_start + jnp.arange(block_rows, dtype=jnp.int32), prefix_lens)
        visible = tok_seg[:, None] == key_seg[None, :]
        key_rows = shard_rows[:, :HEAD]
        value_rows = shard_rows[:, HEAD:]
        scores = jnp.where(
            visible,
            jnp.dot(queries, key_rows.T, preferred_element_type=jnp.float32) * score_scale,
            negative,
        )
        new_max = jnp.maximum(row_max, jnp.max(scores, axis=1))
        factor = jnp.exp(row_max - new_max)
        weights = jnp.where(visible, jnp.exp(scores - new_max[:, None]), 0.0)
        summed = summed * factor[:, None] + jnp.dot(
            weights.astype(jnp.bfloat16), value_rows, preferred_element_type=jnp.float32
        )
        return ((new_max, row_total * factor + jnp.sum(weights, axis=1), summed), None)

    numbers = jnp.arange(all_rows // block_rows, dtype=jnp.int32)
    (row_max, row_total, summed), unused = lax.scan(absorb, start_carry, (numbers, blocks))
    attention = (summed / row_total[:, None]).astype(jnp.bfloat16)
    stream_out = (
        floats
        + lax.psum_scatter(
            jnp.dot(attention, w_out, preferred_element_type=jnp.float32),
            ("tensor", "role"),
            scatter_dimension=0,
            tiled=True,
        )
    ).astype(jnp.bfloat16)
    owned = owner_dev == myself
    owned_count = jnp.sum(owned.astype(jnp.int32))
    starts = jnp.cumsum(span_lens) - span_lens
    first_row = jnp.sum(jnp.where(owned, starts, 0))
    length = jnp.sum(jnp.where(owned, span_lens, 0))
    target = jnp.sum(jnp.where(owned, offsets, 0))
    padded = jnp.concatenate(
        [keyval, jnp.zeros((span_rows, keyval.shape[1]), jnp.bfloat16)], axis=0
    )
    kv_block = lax.dynamic_slice_in_dim(padded, first_row, span_rows, 0)
    before = lax.dynamic_slice_in_dim(decode_cache, target, span_rows, 0)
    keep_new = (row_index < length) & (owned_count > 0)
    written = jnp.where(keep_new[:, None], kv_block, before)
    cache_out = lax.dynamic_update_slice_in_dim(decode_cache, written, target, 0)
    return (stream_out, cache_out)


MESH = pl.DeviceIdType.MESH
F32 = jnp.float32
BF16 = jnp.bfloat16
CW, CCW = 0, 1


def chip_at(position, chips):
    back = position // (chips // 2)
    return (1 - back) * 2 * position + back * (2 * (chips - 1 - position) + 1)


def fused(
    x_ref,
    gain_ref,
    span_ref,
    plen_ref,
    owner_ref,
    offset_ref,
    wq_hbm,
    wkv_hbm,
    wout_hbm,
    pre_hbm,
    dec_hbm,
    out_ref,
    cache_ref,
    wq,
    wkv,
    wout,
    dec,
    normed,
    xsend,
    xrecv,
    kvbuf,
    kvt,
    qall,
    sums_out,
    sums_in,
    scores,
    part,
    peer_out,
    peer_in,
    ring_out,
    ring_in,
    lsem,
    xs,
    xr,
    ags,
    agr,
    pfs,
    pfr,
    p1s,
    p1r,
    p2s,
    p2r,
    pps,
    ppr,
    kvs,
    kvr,
    qs,
    qr,
    ss,
    sr,
    pes,
    per,
    rss,
    rsr,
):
    chips = lax.axis_size("tensor")
    devices = 2 * chips
    t = lax.axis_index("tensor")
    c = lax.axis_index("role")
    peer = 1 - c
    d = 2 * t + c
    odd = t % 2
    pos = (1 - odd) * (t // 2) + odd * (chips - 1 - t // 2)
    nxt = chip_at((pos + 1) % chips, chips)
    prv = chip_at((pos + chips - 1) % chips, chips)
    width = x_ref.shape[1]
    half = width // 2
    quarter = width // 4
    tokens = 16 * chips
    pre_rows = pre_hbm.shape[0]
    g = t // 4
    y = t % 2
    across = t + 1 - 2 * y
    along = t + 2 - 4 * ((t // 2) % 2)

    def remote(src, dst, ssem, rsem, tt, cc):
        return pltpu.make_async_remote_copy(
            src_ref=src,
            dst_ref=dst,
            send_sem=ssem,
            recv_sem=rsem,
            device_id={"tensor": tt, "role": cc},
            device_id_type=MESH,
        )

    sent = []

    def send(*args):
        copy = remote(*args)
        copy.start()
        sent.append(copy)

    barrier = pltpu.get_barrier_semaphore()
    for r in range(1, devices):
        other = (d + r) % devices
        pl.semaphore_signal(
            barrier, inc=1, device_id={"tensor": other // 2, "role": other % 2}, device_id_type=MESH
        )

    def pre_slot(which, row, core):
        index = which * 4 + row * 2 + core
        return kvbuf.at[pl.ds(pl.multiple_of(index * pre_rows, pre_rows), pre_rows), :]

    def head_columns(head):
        return pre_hbm.at[:, pl.ds(pl.multiple_of(head * 2 * HEAD, 2 * HEAD), 2 * HEAD)]

    loads = [
        pltpu.make_async_copy(head_columns(g), pre_slot(0, y, c), lsem.at[0]),
        pltpu.make_async_copy(wkv_hbm, wkv, lsem.at[1]),
        pltpu.make_async_copy(wq_hbm, wq, lsem.at[2]),
        pltpu.make_async_copy(wout_hbm, wout, lsem.at[3]),
        pltpu.make_async_copy(dec_hbm, dec, lsem.at[4]),
    ]
    for load in loads:
        load.start()

    floats = x_ref[...].astype(F32)
    mine = floats * lax.rsqrt(jnp.mean(floats * floats, axis=1, keepdims=True) + epsilon)
    mine = mine * gain_ref[...].astype(F32).reshape(1, width)
    is_one = (c == 1).astype(F32)
    left, right = mine[:, :half], mine[:, half:]
    xsend[...] = jnp.where(is_one > 0.5, left, right).astype(BF16)
    kept = jnp.where(is_one > 0.5, right, left).astype(BF16).astype(F32)

    pl.semaphore_wait(barrier, devices - 1)
    send(xsend, xrecv, xs, xr, t, peer)

    def block(chip, core, h=None):
        column = core * half if h is None else core * half + h * quarter
        size = half if h is None else quarter
        return (
            pl.ds(pl.multiple_of(16 * chip, 16), 16),
            pl.ds(pl.multiple_of(column, quarter), size),
        )

    remote(xsend, xrecv, xs, xr, t, peer).wait_recv()
    theirs = xrecv[...].astype(F32)
    first = jnp.where(is_one > 0.5, theirs, kept)
    second = jnp.where(is_one > 0.5, kept, theirs)
    normed[block(t, c)] = jnp.concatenate([first, second], axis=0).astype(BF16)

    def source(way, hops):
        return chip_at((pos + chips - hops) % chips if way == CW else (pos + hops) % chips, chips)

    def hop(way, s, h):
        here = normed.at[block(source(way, s), c, h)]
        send(here, here, ags.at[way, s, h], agr.at[way, s, h], (nxt, prv)[way], c)

    last = chips // 2 - 1
    own = normed.at[block(t, c)]
    messages = [(s, h, way) for s in range(last + 1) for h in range(2) for way in (CW, CCW)]
    messages = [m for m in messages if m[0] < last or m[1] == m[2]]
    messages = sorted(messages, key=lambda m: (m[0], m[1] != m[2]))
    for s, h, way in messages:
        if s == 0:
            hop(way, 0, h)
    send(own, own, pfs.at[0, last, 1], pfr.at[0, last, 1], t, peer)
    loads[0].wait()

    def spread(which):
        slot = pre_slot(which, y, c)
        send(slot, slot, p2s.at[which], p2r.at[which], across, c)
        send(slot, slot, pps.at[which, 0], ppr.at[which, 0], t, peer)

    for s, h, way in messages:
        landed = normed.at[block(source(way, s + 1), c, h)]
        remote(landed, landed, ags.at[way, s, h], agr.at[way, s, h], nxt, c).wait_recv()
        if (s + 1, h, way) in messages:
            hop(way, s + 1, h)
        send(landed, landed, pfs.at[way, s, h], pfr.at[way, s, h], t, peer)
        if (s, h, way) == (last - 1, 0, CCW):
            send(head_columns(1 - g), pre_slot(1, y, c), p1s, p1r, (t + 4) % chips, c)
            spread(0)

    own = normed.at[block(t, peer)]
    remote(own, own, pfs.at[0, last, 1], pfr.at[0, last, 1], t, peer).wait_recv()
    for s, h, way in messages:
        landed = normed.at[block(source(way, s + 1), peer, h)]
        remote(landed, landed, pfs.at[way, s, h], pfr.at[way, s, h], t, peer).wait_recv()
    loads[1].wait()
    nt = (((1,), (1,)), ((), ()))
    kv = lax.dot_general(wkv[...], normed[...], nt, preferred_element_type=F32)
    kv_rows = wkv.shape[0]

    def kv_slot(index):
        return kvt.at[pl.ds(pl.multiple_of(index * kv_rows, kv_rows), kv_rows), :]

    kv_slot(d)[...] = kv.astype(BF16)
    for r in range(1, devices):
        other = (d + r) % devices
        send(kv_slot(d), kv_slot(d), kvs.at[r], kvr.at[r], other // 2, other % 2)
    loads[2].wait()
    queries = jnp.dot(normed[...], wq[...], preferred_element_type=F32).astype(BF16)
    qall[:tokens, :] = queries
    send(qall.at[pl.ds(0, tokens)], qall.at[pl.ds(tokens, tokens)], qs, qr, along, c)
    slot = pre_slot(1, y, c)
    remote(slot, slot, p1s, p1r, t, peer).wait_recv()
    spread(1)

    def segments(positions, ref):
        end = 0
        total = jnp.zeros_like(positions)
        for r in range(ref.shape[0]):
            end = end + ref[r]
            total = total + (positions >= end).astype(jnp.int32)
        return total

    tok_col = segments(lax.broadcasted_iota(jnp.int32, (tokens, 1), 0), span_ref)
    tok_row = segments(lax.broadcasted_iota(jnp.int32, (1, tokens), 1), span_ref)

    def wait_slot(slot, ssem, rsem):
        remote(slot, slot, ssem, rsem, t, peer).wait_recv()

    score_scale = 1.0 / HEAD**0.5
    tok_two = jnp.concatenate([tok_col, tok_col], axis=0)
    tile = 2 * pre_rows
    seen = []
    tops = None
    wait_slot(pre_slot(0, 1 - y, c), p2s.at[0], p2r.at[0])
    send(pre_slot(0, 1 - y, c), pre_slot(0, 1 - y, c), pps.at[0, 1], ppr.at[0, 1], t, peer)
    remote(
        qall.at[pl.ds(0, tokens)], qall.at[pl.ds(tokens, tokens)], qs, qr, t, peer
    ).wait_recv()
    pieces = [(0, 0), (0, 1), (1, 0), (1, 1)]

    def piece_rows(which, rel):
        chip_row = y if rel == 0 else 1 - y
        return pl.ds(pl.multiple_of((which * 2 + chip_row) * tile, tile), tile)

    for i, (which, rel) in enumerate(pieces):
        chip_row = y if rel == 0 else 1 - y
        if (which, rel) == (1, 1):
            wait_slot(pre_slot(1, chip_row, c), p2s.at[1], p2r.at[1])
            slot = pre_slot(1, chip_row, c)
            send(slot, slot, pps.at[1, 1], ppr.at[1, 1], t, peer)
        wait_slot(pre_slot(which, chip_row, peer), pps.at[which, rel], ppr.at[which, rel])
        chip = (2 * (t // 2) + 4 * which) % chips + chip_row
        seg = segments(lax.broadcasted_iota(jnp.int32, (1, tile), 1) + chip * tile, plen_ref)
        seen.append(seg)
        raw = lax.dot_general(
            qall[...], kvbuf[piece_rows(which, rel), :HEAD], nt, preferred_element_type=F32
        )
        masked = jnp.where(tok_two == seg, raw * score_scale, negative)
        scores[:, i * tile : (i + 1) * tile] = masked
        top = jnp.max(masked, axis=1, keepdims=True)
        tops = top if tops is None else jnp.maximum(tops, top)

    def absorb(first_row):
        rows = slice(first_row, first_row + tokens)
        top = tops[rows]
        total = jnp.zeros((tokens, 1), F32)
        product = jnp.zeros((tokens, HEAD), F32)
        for i, (which, rel) in enumerate(pieces):
            weights = jnp.exp(scores[rows, i * tile : (i + 1) * tile] - top)
            weights = jnp.where(tok_col == seen[i], weights, 0.0)
            total = total + jnp.sum(weights, axis=1, keepdims=True)
            product = product + jnp.dot(
                weights.astype(BF16), kvbuf[piece_rows(which, rel), HEAD:], preferred_element_type=F32
            )
        return top, total, product

    top, total, product = absorb(tokens)
    lane = lax.broadcasted_iota(jnp.int32, (tokens, tokens), 1)
    turned = jnp.transpose(jnp.where(lane < tokens // 2, top, total))
    sums_out[:tokens, :] = product
    sums_out[tokens:, :] = turned[tokens // 2 - 8 : tokens // 2 + 8]
    send(sums_out, sums_in, ss, sr, along, c)
    top, total, product = absorb(0)

    for r in range(1, devices):
        slot = kv_slot((d + devices - r) % devices)
        remote(slot, slot, kvs.at[r], kvr.at[r], t, peer).wait_recv()
    key_base = pl.multiple_of(g * 2 * HEAD, 2 * HEAD)
    span_keys = kvt[pl.ds(key_base, HEAD), :]
    span_values = kvt[pl.ds(key_base + HEAD, HEAD), :]
    before = lax.broadcasted_iota(jnp.int32, (tokens, tokens), 0) >= lax.broadcasted_iota(
        jnp.int32, (tokens, tokens), 1
    )
    span_mask = (tok_col == tok_row) & before
    span_scores = jnp.where(
        span_mask, jnp.dot(queries, span_keys, preferred_element_type=F32) * score_scale, negative
    )
    remote(sums_out, sums_in, ss, sr, t, peer).wait_recv()
    turned = jnp.transpose(jnp.concatenate([sums_in[tokens:, :]] * (tokens // 16), axis=0))
    other_top, other_total = turned[:, 0:1], turned[:, 8:9]
    span_top = jnp.max(span_scores, axis=1, keepdims=True)
    row_max = jnp.maximum(jnp.maximum(top, other_top), span_top)
    weights = jnp.where(span_mask, jnp.exp(span_scores - row_max), 0.0)
    factor, other_factor = jnp.exp(top - row_max), jnp.exp(other_top - row_max)
    row_total = (
        jnp.sum(weights, axis=1, keepdims=True) + total * factor + other_total * other_factor
    )
    summed = lax.dot_general(weights.astype(BF16), span_values, nt, preferred_element_type=F32)
    summed = summed + product * factor + sums_in[:tokens, :] * other_factor
    attention = (summed / row_total).astype(BF16)

    loads[3].wait()
    step = 1024
    for i in range(width // step):
        part[:, i * step : (i + 1) * step] = jnp.dot(
            attention, wout[:, i * step : (i + 1) * step], preferred_element_type=F32
        )

    def stacked(k, core, h):
        rows = pl.ds(pl.multiple_of(16 * chip_at((pos + k) % chips, chips) + 8 * core, 8), 8)
        top = part[rows, h * quarter : (h + 1) * quarter]
        bottom = part[rows, half + h * quarter : half + (h + 1) * quarter]
        return jnp.concatenate([top, bottom], axis=0)

    order = [4, 3, 5, 2, 6, 1, 7, 0]
    for k in order:
        for h in range(2):
            peer_out[k, :, h * quarter : (h + 1) * quarter] = stacked(k, peer, h).astype(BF16)
        send(peer_out.at[k], peer_in.at[k], pes.at[k], per.at[k], t, peer)

    def summand(k, h):
        return stacked(k, c, h) + peer_in[k, :, h * quarter : (h + 1) * quarter].astype(F32)

    def from_peer(k):
        remote(peer_out.at[k], peer_in.at[k], pes.at[k], per.at[k], t, peer).wait_recv()

    def from_ring(way, s, h):
        remote(
            ring_out.at[way, s, h], ring_in.at[way, s, h], rss.at[way, s, h], rsr.at[way, s, h], nxt, c
        ).wait_recv()
        return ring_in[way, s, h].astype(F32)

    hops = [(s, h, way) for s in range(4) for h in range(2) for way in (CW, CCW)]
    hops = [m for m in hops if m[0] > 0 or m[1] == m[2]]
    hops = [m for m in hops if m[0] == 0] + sorted(
        [m for m in hops if m[0] > 0], key=lambda m: (m[0], m[1] == m[2])
    )
    ready = []
    for s, h, way in hops:
        k = 4 - s if way == CW else 4 + s
        if k not in ready:
            from_peer(k)
            ready.append(k)
        value = summand(k, h)
        if (s - 1, h, way) in hops:
            value = value + from_ring(way, s - 1, h)
        ring_out[way, s, h] = value.astype(BF16)
        send(
            ring_out.at[way, s, h],
            ring_in.at[way, s, h],
            rss.at[way, s, h],
            rsr.at[way, s, h],
            (nxt, prv)[way],
            c,
        )

    first_row = 0
    length = 0
    target = 0
    start = 0
    for r in range(span_ref.shape[0]):
        own_it = (owner_ref[r] == d).astype(jnp.int32)
        first_row = first_row + own_it * start
        length = length + own_it * span_ref[r]
        target = target + own_it * offset_ref[r]
        start = start + span_ref[r]
    loads[4].wait()
    cache_rows = dec.shape[0]
    row = lax.broadcasted_iota(jnp.int32, (cache_rows, tokens), 0) - target
    token = lax.broadcasted_iota(jnp.int32, (cache_rows, tokens), 1)
    picks = ((token - first_row) == row) & (row >= 0) & (row < length)
    picked = lax.dot_general(
        picks.astype(F32).astype(BF16), kvt[...], nt, preferred_element_type=F32
    )
    row = lax.broadcasted_iota(jnp.int32, (cache_rows, 1), 0) - target
    written = jnp.where((row >= 0) & (row < length), picked, dec[...].astype(F32))
    cache_ref[...] = written.astype(BF16)

    from_peer(0)
    for h in range(2):
        value = summand(0, h) + from_ring(CW, 3, h) + from_ring(CCW, 3, h)
        for side in range(2):
            columns = slice(side * half + h * quarter, side * half + (h + 1) * quarter)
            out_ref[:, columns] = (
                x_ref[:, columns].astype(F32) + value[8 * side : 8 * side + 8]
            ).astype(BF16)
    for copy in sent:
        copy.wait_send()


def hand_over(stream_ref, cache_ref, stream_out, cache_out, stream_held, cache_held, sems):
    pairs = [
        (stream_ref, stream_held, stream_out),
        (cache_ref, cache_held, cache_out),
    ]
    into = [pltpu.make_async_copy(a, b, sems.at[i]) for i, (a, b, _) in enumerate(pairs)]
    out = [pltpu.make_async_copy(b, e, sems.at[2 + i]) for i, (_, b, e) in enumerate(pairs)]
    for copy in into:
        copy.start()
    for arrival, departure in zip(into, out):
        arrival.wait()
        departure.start()
    for copy in out:
        copy.wait()


def fused_shards(
    stream_in,
    norm_gain,
    w_query,
    w_keyval,
    w_out,
    prefix_cache,
    span_lens,
    prefix_lens,
    owner_dev,
    offsets,
    decode_cache,
):
    chips = lax.axis_size("tensor")
    devices = 2 * chips
    rows, width = stream_in.shape
    tokens = rows * devices
    pre_rows = prefix_cache.shape[0]
    quarter = width // 4
    vmem = pl.BlockSpec(memory_space=pltpu.VMEM)
    smem = pl.BlockSpec(memory_space=pltpu.SMEM)
    hbm = pl.BlockSpec(memory_space=pl.ANY)
    dma = pltpu.SemaphoreType.DMA
    results = pl.pallas_call(
        fused,
        out_shape=(
            jax.ShapeDtypeStruct(stream_in.shape, BF16),
            jax.ShapeDtypeStruct(decode_cache.shape, BF16),
        ),
        in_specs=[vmem, vmem] + [smem] * 4 + [hbm] * 5,
        out_specs=(vmem, vmem),
        scratch_shapes=[
            pltpu.VMEM(w_query.shape, BF16),
            pltpu.VMEM((w_keyval.shape[1], width), BF16),
            pltpu.VMEM(w_out.shape, BF16),
            pltpu.VMEM(decode_cache.shape, BF16),
            pltpu.VMEM((tokens, width), BF16),
            pltpu.VMEM((8, width // 2), BF16),
            pltpu.VMEM((8, width // 2), BF16),
            pltpu.VMEM((devices // 2 * pre_rows, 2 * HEAD), BF16),
            pltpu.VMEM((devices * w_keyval.shape[1], tokens), BF16),
            pltpu.VMEM((2 * tokens, HEAD), BF16),
            pltpu.VMEM((tokens + 16, HEAD), F32),
            pltpu.VMEM((tokens + 16, HEAD), F32),
            pltpu.VMEM((2 * tokens, devices // 2 * pre_rows), F32),
            pltpu.VMEM((tokens, width), F32),
            pltpu.VMEM((chips, 16, width // 2), BF16),
            pltpu.VMEM((chips, 16, width // 2), BF16),
            pltpu.VMEM((2, 4, 2, 16, quarter), BF16),
            pltpu.VMEM((2, 4, 2, 16, quarter), BF16),
            dma((5,)),
            dma,
            dma,
            dma((2, 4, 2)),
            dma((2, 4, 2)),
            dma((2, 4, 2)),
            dma((2, 4, 2)),
            dma,
            dma,
            dma((2,)),
            dma((2,)),
            dma((2, 2)),
            dma((2, 2)),
            dma((devices,)),
            dma((devices,)),
            dma,
            dma,
            dma,
            dma,
            dma((chips,)),
            dma((chips,)),
            dma((2, 4, 2)),
            dma((2, 4, 2)),
        ],
        compiler_params=pltpu.CompilerParams(
            collective_id=0, has_side_effects=True, vmem_limit_bytes=60 * 1024 * 1024
        ),
        name="fused_attention",
    )(
        stream_in,
        norm_gain,
        span_lens,
        prefix_lens,
        owner_dev,
        offsets,
        w_query,
        w_keyval.T,
        w_out,
        prefix_cache,
        decode_cache,
    )
    return pl.pallas_call(
        hand_over,
        out_shape=(
            jax.ShapeDtypeStruct(stream_in.shape, BF16),
            jax.ShapeDtypeStruct(decode_cache.shape, BF16),
        ),
        in_specs=[hbm, hbm],
        out_specs=(hbm, hbm),
        scratch_shapes=[
            pltpu.VMEM(stream_in.shape, BF16),
            pltpu.VMEM(decode_cache.shape, BF16),
            dma((4,)),
        ],
        name="hand_over",
    )(*results)


def solution(mesh):
    in_specs = (
        P(("groups", "tensor", "role"), None),
        P(),
        P(None, ("tensor", "role")),
        P(None, ("tensor", "role")),
        P(("tensor", "role"), None),
        P(("groups", "tensor", "role"), None),
        P("groups"),
        P("groups"),
        P("groups"),
        P("groups"),
        P(("groups", "tensor", "role"), None),
    )
    out_specs = (P(("groups", "tensor", "role"), None), P(("groups", "tensor", "role"), None))
    small = mesh.shape["tensor"] == 8 and mesh.shape["role"] == 2
    body = fused_shards if small else shards
    return jax.shard_map(body, mesh=mesh, in_specs=in_specs, out_specs=out_specs, check_vma=False)
```
